32 devices in a mesh: row: 4 (over x, core), col: 4 (over z), pair: 2 (over y).
Axes of the slice: x: 2, y: 2, z: 4, core: 2. Of those that a mesh axis runs over, the one named last changes fastest.
Arguments:
- factors: bfloat16 [1800, 512, 16], P('pair', ('row', 'col')), may hold values from -1 to 1
- amplitudes: bfloat16 [20, 16, 16], P('pair'), may hold values from -0.796875 to 0.796875
- virt_irreps: int32 [512], replicated, may hold values from 0 to 3
- win_irreps: int32 [16], replicated, may hold values from 0 to 3
- occ_irreps: int32 [120], replicated, may hold values from 0 to 3
- pair_list: int32 [20, 2], replicated, may hold values from 0 to 119
Outputs:
- ladder: float32 [20, 512, 4, 128], P('pair', 'row', None, 'col')
The draws below stay inside these ranges and needn't reach their ends.
All inputs are finite; a program needn't handle non-finite values.
Results may differ from the reference program's by a relative error of at most 0.0003.
Values may be sent and summed in bfloat16 or wider, within the bound.
No kernel may reach another device: no remote copies, remote signals or barrier semaphores. Data moves between devices by JAX's collectives and lax.ppermute only.
A program may use at most 64 MiB of HBM per device.

```python
import jax
import jax.numpy as jnp
from jax import lax

NAUX = 1800
NV = 512
NOCC = 120
CW = 16
PAIRS = 20
N_ROW = 4


def set_ends(entries, stream_key, smallest, top_value):
    shape = entries.shape
    place = [jax.random.randint(jax.random.fold_in(stream_key, axis), (), 0, shape[axis]) for axis in range(len(shape))]
    entries = entries.at[tuple(place)].set(smallest)
    longest = shape.index(max(shape))
    place[longest] = (place[longest] + 1) % shape[longest]
    return entries.at[tuple(place)].set(top_value)


def levels(key, shape, cuts, least, top_value):
    def one(dim, shards_of):
        draws = jax.random.uniform(jax.random.fold_in(jax.random.fold_in(key, 6), dim), (shards_of,), jnp.float32, least / len(cuts), top_value / len(cuts))
        return jnp.repeat(jnp.exp(draws), shape[dim] // shards_of).reshape((-1,) + (1,) * (len(shape) - dim - 1))

    gain = one(*cuts[0])
    for cut in cuts[1:]:
        gain = gain * one(*cut)
    return gain


def gaussian(stream_key, dims, scale, reach, cuts=(), held_as=jnp.bfloat16):
    entries = scale * jax.random.normal(stream_key, dims, jnp.float32)
    if cuts:
        entries = entries * levels(stream_key, dims, cuts, -0.22, 0.18)
    return jnp.clip(entries, -reach, reach).astype(held_as)


def setup_inputs(seed: int = 0) -> dict:
    splits = jax.random.split(jax.random.key(seed), 7)
    factors = gaussian(splits[0], (NAUX, NV, CW), 0.15, 1.0, ((0, 2), (1, 16)))
    amplitudes = gaussian(splits[1], (PAIRS, CW, CW), 0.125, 0.796875, ((0, 2),))
    virt_irreps = set_ends(jax.random.randint(splits[2], (NV,), 0, 4), jax.random.fold_in(splits[2], 1), 0, 3).astype(jnp.int32)
    win_irreps = set_ends(jax.random.randint(splits[3], (CW,), 0, 4), jax.random.fold_in(splits[3], 1), 0, 3).astype(jnp.int32)
    occ_irreps = set_ends(jax.random.randint(splits[4], (NOCC,), 0, 4), jax.random.fold_in(splits[4], 1), 0, 3).astype(jnp.int32)
    pair_list = set_ends(jax.random.randint(splits[5], (PAIRS, 2), 0, NOCC), jax.random.fold_in(splits[5], 1), 0, NOCC - 1).astype(jnp.int32)
    return dict(factors=factors, amplitudes=amplitudes, virt_irreps=virt_irreps, win_irreps=win_irreps, occ_irreps=occ_irreps, pair_list=pair_list)


def reference(factors, amplitudes, virt_irreps, win_irreps, occ_irreps, pair_list):
    first = occ_irreps[pair_list[:, 0]]
    second = occ_irreps[pair_list[:, 1]]
    symmetry = jnp.bitwise_xor(first, second)
    product = jnp.bitwise_xor(win_irreps[:, None], win_irreps[None, :])
    weights = jnp.where(product[None, :, :] == symmetry[:, None, None], amplitudes.astype(jnp.float32), 0.0)
    block_rows = min(64, NV)
    columns = factors.reshape(NAUX, NV * CW)

    def one_block(index):
        rows = lax.dynamic_slice_in_dim(factors, index * block_rows, block_rows, 1).reshape(NAUX, block_rows * CW)
        integral = lax.dot_general(rows, columns, (((0,), (0,)), ((), ())), preferred_element_type=jnp.float32)
        integral = integral.reshape(block_rows, CW, NV, CW)
        return jnp.einsum("acbd,pcd->pab", integral.astype(jnp.float32), weights, precision=lax.Precision.HIGHEST)

    blocks = lax.map(one_block, jnp.arange(NV // block_rows, dtype=jnp.int32))
    full = jnp.transpose(blocks, (1, 0, 2, 3)).reshape(PAIRS, NV, NV)
    pair_sym = jnp.bitwise_xor(virt_irreps[:, None], virt_irreps[None, :])
    result = jnp.where(pair_sym[None, :, :] == symmetry[:, None, None], full, 0.0)
    return result.reshape(PAIRS, NV, N_ROW, NV // N_ROW)
```

```python
import functools

import jax
import jax.numpy as jnp
from jax import lax
from jax.experimental import pallas as pl
from jax.experimental.pallas import tpu as pltpu
from jax.sharding import PartitionSpec as P

VMEM_LIMIT = 40 * 1024 * 1024
NT = (((1,), (1,)), ((), ()))
NN = (((1,), (0,)), ((), ()))


def lookup_symmetry(occ_irreps, pair_list):
    labels = jnp.arange(occ_irreps.shape[0], dtype=jnp.int32)
    onehot = pair_list[:, :, None] == labels[None, None, :]
    picked = jnp.sum(jnp.where(onehot, occ_irreps[None, None, :], 0), axis=-1)
    return jnp.bitwise_xor(picked[:, 0], picked[:, 1])


def mask_amplitudes(amplitudes, win_irreps, symmetry):
    product = jnp.bitwise_xor(win_irreps[:, None], win_irreps[None, :])
    allowed = product[None, :, :] == symmetry[:, None, None]
    return jnp.where(allowed, amplitudes, jnp.zeros_like(amplitudes))


def gathered_body(factors, amplitudes, virt_irreps, win_irreps, occ_irreps, pair_list):
    per_device = factors.shape[1]
    n_rows = lax.axis_size("row")
    n_cols = lax.axis_size("col")
    block_a = per_device * n_cols
    slab = amplitudes.shape[0]
    symmetry = lookup_symmetry(occ_irreps, pair_list)
    own_symmetry = lax.dynamic_slice_in_dim(symmetry, lax.axis_index("pair") * slab, slab)
    every = lax.all_gather(amplitudes, "pair", axis=0, tiled=True)
    weights = mask_amplitudes(every, win_irreps, symmetry).astype(jnp.float32)
    n_fitting, _, width = factors.shape
    b_rows = lax.all_gather(factors, "row", axis=1, tiled=True)
    a_rows = lax.all_gather(factors, "col", axis=1, tiled=True)
    integral = lax.dot_general(
        a_rows.reshape(n_fitting, block_a * width),
        b_rows.reshape(n_fitting, n_rows * per_device * width),
        (((0,), (0,)), ((), ())),
        preferred_element_type=jnp.float32,
    )
    integral = integral.reshape(block_a, width, n_rows * per_device, width)
    part = jnp.einsum("acbd,pcd->pab", integral, weights, precision=lax.Precision.HIGHEST)
    full = lax.psum_scatter(part, "pair", scatter_dimension=0, tiled=True)
    full = full.reshape(slab, block_a, n_rows, per_device)
    a_labels = lax.dynamic_slice_in_dim(virt_irreps, lax.axis_index("row") * block_a, block_a)
    b_labels = lax.dynamic_slice_in_dim(
        virt_irreps.reshape(n_rows, -1), lax.axis_index("col") * per_device, per_device, 1
    )
    pair_sym = jnp.bitwise_xor(a_labels[:, None, None], b_labels[None, :, :])
    allowed = pair_sym[None, :, :, :] == own_symmetry[:, None, None, None]
    return jnp.where(allowed, full, 0.0)


def is_middle():
    col = lax.axis_index("col")
    return jnp.logical_or(col == 1, col == 2)


def window_major(width, per_device):
    n = width * per_device
    into = lax.broadcasted_iota(jnp.int32, (n, n), 0)
    out_of = lax.broadcasted_iota(jnp.int32, (n, n), 1)
    wanted = lax.rem(into, per_device) * width + lax.div(into, per_device)
    return (wanted == out_of).astype(jnp.bfloat16)


def place_rows(panel, order, rows, k):
    width, _, per_device, n_fit = panel.shape
    moved = lax.dot_general(order, rows, NN, preferred_element_type=jnp.float32)
    panel[:, pl.ds(k, 1)] = moved.astype(panel.dtype).reshape(width, 1, per_device, n_fit)


def contract_block(rows, panel, weights, split, sums, keep, send):
    width, n_rows, per_device, n_fit = panel.shape
    n_b = n_rows * per_device
    n_a = rows.shape[0] // width
    half = keep.shape[0]
    n_p = weights.shape[0]

    def integrals(step, carry):
        two = panel[pl.ds(2 * step, 2)].reshape(2 * n_b, n_fit)
        acc = lax.dot_general(rows[...], two, NT, preferred_element_type=jnp.float32)
        high = acc.astype(jnp.bfloat16)
        low = (acc - high.astype(jnp.float32)).astype(jnp.bfloat16)
        for j in range(2):
            lanes = slice(j * n_b, (j + 1) * n_b)
            split[:, 0, pl.ds(2 * step + j, 1)] = high[:, lanes].reshape(n_a, 1, width, n_b)
            split[:, 1, pl.ds(2 * step + j, 1)] = low[:, lanes].reshape(n_a, 1, width, n_b)
        return carry

    lax.fori_loop(0, width // 2, integrals, 0)

    def ladder(step, carry):
        depth = 2 * width * width
        two = [split[2 * step + j].reshape(depth, n_b) for j in range(2)]
        both = jnp.concatenate(two, axis=1)
        res = lax.dot_general(weights[...], both, NN, preferred_element_type=jnp.float32)
        for j in range(2):
            sums[pl.ds((2 * step + j) * n_p, n_p), :] = res[:, j * n_b : (j + 1) * n_b]
        return carry

    lax.fori_loop(0, n_a // 2, ladder, 0)
    for p in range(half):
        keep[p] = sums[pl.ds(p, n_a, stride=n_p), :]
        send[p] = sums[pl.ds(n_p // 2 + p, n_a, stride=n_p), :]


def early_kernel(own, facing, middle, by_core, by_x, by_both, weights, keep, send, panel_out, panel, held, split, sums, sems):
    sources = (own, by_core, by_x, by_both, facing, middle)
    copies = [pltpu.make_async_copy(src, held.at[i], sems.at[i]) for i, src in enumerate(sources)]
    for copy in copies:
        copy.start()
    row = lax.axis_index("row")
    width, _, per_device, _ = panel.shape
    order = window_major(width, per_device)
    for i in range(4):
        copies[i].wait()
        place_rows(panel, order, held[i], jnp.bitwise_xor(row, i))
    back = pltpu.make_async_copy(panel, panel_out, sems.at[6])
    back.start()
    copies[4].wait()
    copies[5].wait()
    contract_block(held.at[0], panel, weights, split, sums, keep.at[0], send.at[0])
    contract_block(held.at[4], panel, weights, split, sums, keep.at[1], send.at[1])

    @pl.when(is_middle())
    def _():
        contract_block(held.at[5], panel, weights, split, sums, keep.at[2], send.at[2])

    back.wait()


def across_kernel(far, facing, by_core, by_x, by_both, weights, keep, send, panel, held, split, sums, sems):
    @pl.when(is_middle())
    def _():
        sources = (facing, by_core, by_x, by_both, far)
        copies = [pltpu.make_async_copy(src, held.at[i], sems.at[i]) for i, src in enumerate(sources)]
        for copy in copies:
            copy.start()
        row = lax.axis_index("row")
        width, _, per_device, _ = panel.shape
        order = window_major(width, per_device)
        for i in range(4):
            copies[i].wait()
            place_rows(panel, order, held[i], jnp.bitwise_xor(row, i))
        copies[4].wait()
        contract_block(held.at[4], panel, weights, split, sums, keep, send)


def late_kernel(far, passed, panel_in, weights, keep, send, panel, held, split, sums, sems):
    copy_panel = pltpu.make_async_copy(panel_in, panel, sems.at[0])
    copy_panel.start()

    @pl.when(is_middle())
    def _():
        copy = pltpu.make_async_copy(far, held, sems.at[1])
        copy.start()
        copy.wait()

    @pl.when(jnp.logical_not(is_middle()))
    def _():
        copy = pltpu.make_async_copy(passed, held, sems.at[1])
        copy.start()
        copy.wait()

    copy_panel.wait()
    contract_block(held, panel, weights, split, sums, keep, send)


def finish_kernel(symmetry, pair_sym, keep_early, got_early, keep_late, got_late, across, out, whole):
    col = lax.axis_index("col")
    middle = is_middle()
    lower = col < 2
    n_p, n_a, _ = keep_late.shape
    planes = (col, jnp.bitwise_xor(col, 1), jnp.where(lower, 2, 1), jnp.where(lower, 3, 0))

    def place(s):
        return pl.ds(pl.multiple_of(planes[s] * n_a, n_a), n_a)

    for s in range(2):
        whole[:, place(s), :] = keep_early[s] + got_early[s]

    @pl.when(middle)
    def _():
        whole[:, place(2), :] = keep_early[2] + got_early[2]
        whole[:, place(3), :] = keep_late[...] + got_late[...]

    @pl.when(jnp.logical_not(middle))
    def _():
        whole[:, place(2), :] = keep_late[...] + got_late[...]
        whole[:, place(3), :] = across[...]

    for p in range(n_p):
        out[p] = jnp.where(pair_sym[...] == symmetry[p], whole[p].T, 0.0)


def swap(array, axis, mask):
    size = lax.axis_size(axis)
    return lax.ppermute(array, axis, [(i, i ^ mask) for i in range(size)])


def staged_body(factors, amplitudes, virt_irreps, win_irreps, occ_irreps, pair_list):
    n_fit, per_device, width = factors.shape
    n_rows = lax.axis_size("row")
    n_cols = lax.axis_size("col")
    n_b = n_rows * per_device
    block_a = per_device * n_cols
    slab = amplitudes.shape[0]
    rows_shape = (per_device * width, n_fit)

    own = jnp.transpose(factors, (1, 2, 0)).reshape(rows_shape)
    facing = swap(own, "col", 1)
    middle = lax.ppermute(own, "col", [(1, 2), (2, 1)])
    by_x = swap(own, "row", 2)
    by_core = swap(own, "row", 1)
    other_amplitudes = swap(amplitudes, "pair", 1)

    far = lax.ppermute(facing, "col", [(1, 2), (2, 1)])
    passed = lax.ppermute(middle, "col", [(1, 0), (2, 3)])
    by_both = swap(by_x, "row", 1)

    def middle_swap(array, mask):
        pairs = [(r * n_cols + c, (r ^ mask) * n_cols + c) for r in range(n_rows) for c in (1, 2)]
        return lax.ppermute(array, ("row", "col"), pairs)

    facing_x = middle_swap(facing, 2)
    facing_core = middle_swap(facing, 1)
    facing_both = middle_swap(facing_x, 1)

    symmetry = lookup_symmetry(occ_irreps, pair_list)
    pair_index = lax.axis_index("pair")
    own_symmetry = lax.dynamic_slice_in_dim(symmetry, pair_index * slab, slab)
    other_symmetry = lax.dynamic_slice_in_dim(symmetry, (1 - pair_index) * slab, slab)
    padded = 16 * pl.cdiv(slab, 16)

    def weight_rows(array, sym):
        masked = jnp.transpose(mask_amplitudes(array, win_irreps, sym), (0, 2, 1)).reshape(slab, width * width)
        return jnp.pad(jnp.concatenate([masked, masked], axis=1), ((0, padded - slab), (0, 0)))

    weights = jnp.concatenate(
        [weight_rows(amplitudes, own_symmetry), weight_rows(other_amplitudes, other_symmetry)], axis=0
    )

    a_labels = lax.dynamic_slice_in_dim(virt_irreps, lax.axis_index("row") * block_a, block_a)
    b_labels = lax.dynamic_slice_in_dim(
        virt_irreps.reshape(n_rows, -1), lax.axis_index("col") * per_device, per_device, 1
    ).reshape(n_b)
    pair_sym = jnp.bitwise_xor(b_labels[:, None], a_labels[None, :])

    anywhere = pl.BlockSpec(memory_space=pl.ANY)
    vmem = pl.BlockSpec(memory_space=pltpu.VMEM)
    smem = pl.BlockSpec(memory_space=pltpu.SMEM)
    params = pltpu.CompilerParams(vmem_limit_bytes=VMEM_LIMIT)
    block = jax.ShapeDtypeStruct((slab, per_device, n_b), jnp.float32)
    blocks = jax.ShapeDtypeStruct((3, slab, per_device, n_b), jnp.float32)
    panel_shape = (width, n_rows, per_device, n_fit)
    panel_scratch = pltpu.VMEM(panel_shape, jnp.bfloat16)
    split_scratch = pltpu.VMEM((per_device, 2, width, width, n_b), jnp.bfloat16)
    sums_scratch = pltpu.VMEM((per_device * 2 * padded, n_b), jnp.float32)

    def cost(n_blocks):
        flops = 2 * n_blocks * rows_shape[0] * n_b * width * n_fit
        return pl.CostEstimate(flops=flops, bytes_accessed=8 * rows_shape[0] * n_fit, transcendentals=0)

    keep_early, send_early, panel = pl.pallas_call(
        early_kernel,
        out_shape=(blocks, blocks, jax.ShapeDtypeStruct(panel_shape, jnp.bfloat16)),
        in_specs=[anywhere] * 6 + [vmem],
        out_specs=(vmem, vmem, anywhere),
        scratch_shapes=[
            panel_scratch,
            pltpu.VMEM((6,) + rows_shape, jnp.bfloat16),
            split_scratch,
            sums_scratch,
            pltpu.SemaphoreType.DMA((7,)),
        ],
        compiler_params=params,
        cost_estimate=cost(4),
    )(own, facing, middle, by_core, by_x, by_both, weights)
    got_early = swap(send_early, "pair", 1)

    keep_across, send_across = pl.pallas_call(
        across_kernel,
        out_shape=(block, block),
        in_specs=[anywhere] * 5 + [vmem],
        out_specs=(vmem, vmem),
        scratch_shapes=[
            panel_scratch,
            pltpu.VMEM((5,) + rows_shape, jnp.bfloat16),
            split_scratch,
            sums_scratch,
            pltpu.SemaphoreType.DMA((5,)),
        ],
        compiler_params=params,
        cost_estimate=cost(1),
    )(far, facing, facing_core, facing_x, facing_both, weights)
    n_pair = lax.axis_size("pair")
    across_pairs = [(c * n_pair + y, c * n_pair + (y ^ 1)) for c in (1, 2) for y in range(n_pair)]
    got_across = lax.ppermute(send_across, ("col", "pair"), across_pairs)
    across = lax.ppermute(keep_across + got_across, "col", [(1, 0), (2, 3)])

    keep_late, send_late = pl.pallas_call(
        late_kernel,
        out_shape=(block, block),
        in_specs=[anywhere] * 3 + [vmem],
        out_specs=(vmem, vmem),
        scratch_shapes=[
            panel_scratch,
            pltpu.VMEM(rows_shape, jnp.bfloat16),
            split_scratch,
            sums_scratch,
            pltpu.SemaphoreType.DMA((2,)),
        ],
        compiler_params=params,
        cost_estimate=cost(1),
    )(far, passed, panel, weights)
    got_late = swap(send_late, "pair", 1)

    out = pl.pallas_call(
        finish_kernel,
        out_shape=jax.ShapeDtypeStruct((slab, n_b, block_a), jnp.float32),
        in_specs=[smem] + [vmem] * 6,
        out_specs=vmem,
        scratch_shapes=[pltpu.VMEM((slab, block_a, n_b), jnp.float32)],
        compiler_params=params,
    )(own_symmetry, pair_sym, keep_early, got_early, keep_late, got_late, across)
    return jnp.transpose(out.reshape(slab, n_rows, per_device, block_a), (0, 3, 1, 2))


def solution(mesh):
    staged = (mesh.shape["row"], mesh.shape["col"], mesh.shape["pair"]) == (4, 4, 2)
    body = staged_body if staged else gathered_body
    in_specs = (P("pair", ("row", "col"), None), P("pair", None, None), P(), P(), P(), P())
    out_specs = P("pair", "row", None, "col")
    return jax.shard_map(body, mesh=mesh, in_specs=in_specs, out_specs=out_specs, check_vma=False)
```

```python
import jax
import jax.numpy as jnp
from jax import lax
from jax.experimental import pallas as pl
from jax.experimental.pallas import tpu as pltpu
from jax.sharding import PartitionSpec as P

VMEM_LIMIT = 24 * 1024 * 1024
LANES = 128
NT = (((1,), (1,)), ((), ()))
NN = (((1,), (0,)), ((), ()))
TN = (((0,), (0,)), ((), ()))


def lookup_symmetry(occ_irreps, pair_list):
    labels = jnp.arange(occ_irreps.shape[0], dtype=jnp.int32)
    onehot = pair_list[:, :, None] == labels[None, None, :]
    picked = jnp.sum(jnp.where(onehot, occ_irreps[None, None, :], 0), axis=-1)
    return jnp.bitwise_xor(picked[:, 0], picked[:, 1])


def mask_amplitudes(amplitudes, win_irreps, symmetry):
    product = jnp.bitwise_xor(win_irreps[:, None], win_irreps[None, :])
    allowed = product[None, :, :] == symmetry[:, None, None]
    return jnp.where(allowed, amplitudes, jnp.zeros_like(amplitudes))


def gathered_body(factors, amplitudes, virt_irreps, win_irreps, occ_irreps, pair_list):
    per_device = factors.shape[1]
    n_rows = lax.axis_size("row")
    n_cols = lax.axis_size("col")
    block_a = per_device * n_cols
    slab = amplitudes.shape[0]
    symmetry = lookup_symmetry(occ_irreps, pair_list)
    own_symmetry = lax.dynamic_slice_in_dim(symmetry, lax.axis_index("pair") * slab, slab)
    every = lax.all_gather(amplitudes, "pair", axis=0, tiled=True)
    weights = mask_amplitudes(every, win_irreps, symmetry).astype(jnp.float32)
    n_fitting, _, width = factors.shape
    b_rows = lax.all_gather(factors, "row", axis=1, tiled=True)
    a_rows = lax.all_gather(factors, "col", axis=1, tiled=True)
    integral = lax.dot_general(
        a_rows.reshape(n_fitting, block_a * width),
        b_rows.reshape(n_fitting, n_rows * per_device * width),
        (((0,), (0,)), ((), ())),
        preferred_element_type=jnp.float32,
    )
    integral = integral.reshape(block_a, width, n_rows * per_device, width)
    part = jnp.einsum("acbd,pcd->pab", integral, weights, precision=lax.Precision.HIGHEST)
    full = lax.psum_scatter(part, "pair", scatter_dimension=0, tiled=True)
    full = full.reshape(slab, block_a, n_rows, per_device)
    a_labels = lax.dynamic_slice_in_dim(virt_irreps, lax.axis_index("row") * block_a, block_a)
    b_labels = lax.dynamic_slice_in_dim(
        virt_irreps.reshape(n_rows, -1), lax.axis_index("col") * per_device, per_device, 1
    )
    pair_sym = jnp.bitwise_xor(a_labels[:, None, None], b_labels[None, :, :])
    allowed = pair_sym[None, :, :, :] == own_symmetry[:, None, None, None]
    return jnp.where(allowed, full, 0.0)


def is_middle():
    col = lax.axis_index("col")
    return jnp.logical_or(col == 1, col == 2)


def one_hot(shape, wanted):
    first = lax.broadcasted_iota(jnp.int32, shape, 0)
    second = lax.broadcasted_iota(jnp.int32, shape, 1)
    return wanted(first, second).astype(jnp.bfloat16)


def multiply(left, right, dims):
    return lax.dot_general(left, right, dims, preferred_element_type=jnp.float32)


def pack_kernel(rest, own, out):
    n, n_fit = own.shape
    whole = n_fit - rest
    out[:n, :] = own[:, :whole]
    below = out.shape[0] - n
    turned = jnp.zeros((below, LANES), jnp.float32)
    for j in range(n // LANES):
        pick = one_hot((below, rest), lambda r, q: r == j * rest + q)
        turned = turned + multiply(pick, own[j * LANES : (j + 1) * LANES, whole:], NT)
    out[n:, :] = jnp.zeros((below, whole), jnp.bfloat16)
    out[n:, :LANES] = turned.astype(jnp.bfloat16)


def fetch(packed, rows, tail, sems):
    n, depth = rows.shape
    whole = depth - LANES
    copies = (
        pltpu.make_async_copy(packed.at[pl.ds(0, n)], rows.at[:, pl.ds(0, whole)], sems.at[0]),
        pltpu.make_async_copy(packed.at[pl.ds(n, tail.shape[0]), pl.ds(0, LANES)], tail, sems.at[1]),
    )
    for copy in copies:
        copy.start()
    return copies


def unpack(copies, rows, tail, rest):
    for copy in copies:
        copy.wait()
    n, depth = rows.shape
    for j in range(n // LANES):
        pick = one_hot(tail.shape, lambda r, q: jnp.logical_and(r == j * rest + q, q < rest))
        back = multiply(tail[...], pick, TN).astype(jnp.bfloat16)
        rows[j * LANES : (j + 1) * LANES, depth - LANES :] = back


def window_major(width, per_device):
    n = width * per_device
    return one_hot((n, n), lambda i, j: lax.rem(i, per_device) * width + lax.div(i, per_device) == j)


def place_rows(panel, order, rows, k):
    width, _, per_device, depth = panel.shape
    moved = multiply(order, rows[...], NN).astype(panel.dtype)
    panel[:, pl.ds(k, 1)] = moved.reshape(width, 1, per_device, depth)


def contract_block(rows, panel, weights, split, sums, keep, send):
    width, n_rows, per_device, depth = panel.shape
    n_b = n_rows * per_device
    n_a = rows.shape[0] // width
    half = keep.shape[0]
    n_p = weights.shape[0]

    def integrals(step, carry):
        two = panel[pl.ds(2 * step, 2)].reshape(2 * n_b, depth)
        acc = multiply(rows[...], two, NT)
        high = acc.astype(jnp.bfloat16)
        low = (acc - high.astype(jnp.float32)).astype(jnp.bfloat16)
        for j in range(2):
            lanes = slice(j * n_b, (j + 1) * n_b)
            split[:, 0, pl.ds(2 * step + j, 1)] = high[:, lanes].reshape(n_a, 1, width, n_b)
            split[:, 1, pl.ds(2 * step + j, 1)] = low[:, lanes].reshape(n_a, 1, width, n_b)
        return carry

    lax.fori_loop(0, width // 2, integrals, 0, unroll=True)

    def ladder(step, carry):
        two = [split[2 * step + j].reshape(2 * width * width, n_b) for j in range(2)]
        res = multiply(weights[...], jnp.concatenate(two, axis=1), NN)
        for j in range(2):
            sums[pl.ds((2 * step + j) * n_p, n_p), :] = res[:, j * n_b : (j + 1) * n_b]
        return carry

    lax.fori_loop(0, n_a // 2, ladder, 0, unroll=True)
    for p in range(half):
        keep[p] = sums[pl.ds(p, n_a, stride=n_p), :]
        send[p] = sums[pl.ds(n_p // 2 + p, n_a, stride=n_p), :]


def pair_symmetry(occ, pairs, p):
    return jnp.bitwise_xor(occ[pairs[0, p]], occ[pairs[1, p]])


def weight_rows(amplitudes, win, occ, pairs, first, n_p):
    n, width = amplitudes.shape
    slab = n // width
    lanes = width * width
    spread = multiply(amplitudes[...], one_hot((width, lanes), lambda d, l: d == lax.div(l, width)), NN)
    c_of_row = lax.rem(lax.broadcasted_iota(jnp.int32, (n, lanes), 0), width)
    c_of_lane = lax.rem(lax.broadcasted_iota(jnp.int32, (n, lanes), 1), width)
    spread = jnp.where(c_of_row == c_of_lane, spread, 0.0).astype(jnp.bfloat16)
    gathered = multiply(one_hot((n_p, n), lambda p, r: p == lax.div(r, width)), spread, NN)
    lane = lax.broadcasted_iota(jnp.int32, (n_p, lanes), 1)
    row = lax.broadcasted_iota(jnp.int32, (n_p, lanes), 0)
    product = jnp.zeros((n_p, lanes), jnp.int32)
    for w in range(width):
        label = win[w]
        product = jnp.bitwise_xor(product, jnp.where(lax.div(lane, width) == w, label, 0))
        product = jnp.bitwise_xor(product, jnp.where(lax.rem(lane, width) == w, label, 0))
    wanted = jnp.full((n_p, lanes), -1, jnp.int32)
    for p in range(slab):
        wanted = jnp.where(row == p, pair_symmetry(occ, pairs, first + p), wanted)
    masked = jnp.where(product == wanted, gathered, 0.0).astype(jnp.bfloat16)
    return jnp.concatenate([masked, masked], axis=1)


def early_kernel(
    rest, own, by_core, by_x, by_both, facing, turned, mine, others, win, occ, pairs,
    keep, send, panel_out, weights, panel, held, tails, split, sums, sems, panel_sem,
):
    middle = is_middle()
    row = lax.axis_index("row")
    width, _, per_device, _ = panel.shape
    sources = (own, by_core, None, by_both, facing, turned)
    copies = [
        None if src is None else fetch(src, held.at[i], tails.at[i], sems.at[i]) for i, src in enumerate(sources)
    ]

    @pl.when(middle)
    def _():
        fetch(by_x, held.at[2], tails.at[2], sems.at[2])

    @pl.when(jnp.logical_not(middle))
    def _():
        fetch(turned, held.at[2], tails.at[2], sems.at[2])

    copies[2] = wait_only(by_x, held.at[2], tails.at[2], sems.at[2])
    slab = mine.shape[0] // width
    n_p = weights.shape[0] // 2
    pair = lax.axis_index("pair")
    weights[:n_p] = weight_rows(mine, win, occ, pairs, pair * slab, n_p)
    weights[n_p:] = weight_rows(others, win, occ, pairs, (1 - pair) * slab, n_p)
    order = window_major(width, per_device)
    for i in range(4):
        unpack(copies[i], held.at[i], tails.at[i], rest)
        place_rows(panel, order, held.at[i], jnp.bitwise_xor(row, i))
    back = pltpu.make_async_copy(panel, panel_out, panel_sem)
    back.start()
    for i in (4, 5):
        unpack(copies[i], held.at[i], tails.at[i], rest)

    def block(s, carry):
        contract_block(held.at[jnp.where(s == 0, 0, 3 + s)], panel, weights, split, sums, keep.at[s], send.at[s])
        return carry

    lax.fori_loop(0, jnp.where(middle, 3, 2), block, 0)
    back.wait()


def wait_only(packed, rows, tail, sems):
    n, depth = rows.shape
    return (
        pltpu.make_async_copy(packed.at[pl.ds(0, n)], rows.at[:, pl.ds(0, depth - LANES)], sems.at[0]),
        pltpu.make_async_copy(packed.at[pl.ds(n, tail.shape[0]), pl.ds(0, LANES)], tail, sems.at[1]),
    )


def across_kernel(
    rest, far, facing, by_core, by_x, by_both, weights, keep, send, panel, held, tails, split, sums, sems
):
    @pl.when(is_middle())
    def _():
        sources = (facing, by_core, by_x, by_both, far)
        copies = [fetch(src, held.at[i], tails.at[i], sems.at[i]) for i, src in enumerate(sources)]
        row = lax.axis_index("row")
        width, _, per_device, _ = panel.shape
        order = window_major(width, per_device)
        for i in range(4):
            unpack(copies[i], held.at[i], tails.at[i], rest)
            place_rows(panel, order, held.at[i], jnp.bitwise_xor(row, i))
        unpack(copies[4], held.at[4], tails.at[4], rest)
        contract_block(held.at[4], panel, weights, split, sums, keep, send)


def late_kernel(rest, far, passed, panel_in, weights, keep, send, panel, held, tail, split, sums, sems, panel_sem):
    copy_panel = pltpu.make_async_copy(panel_in, panel, panel_sem)
    copy_panel.start()
    middle = is_middle()

    @pl.when(middle)
    def _():
        fetch(far, held, tail, sems)

    @pl.when(jnp.logical_not(middle))
    def _():
        fetch(passed, held, tail, sems)

    unpack(wait_only(far, held, tail, sems), held, tail, rest)
    copy_panel.wait()
    contract_block(held, panel, weights, split, sums, keep, send)


def finish_kernel(
    virt, occ, pairs, keep_early, got_early, keep_late, got_late, across, across_other, out, whole
):
    row = lax.axis_index("row")
    col = lax.axis_index("col")
    middle = is_middle()
    lower = col < 2
    n_p, n_a, n_b = keep_late.shape
    planes = (col, jnp.bitwise_xor(col, 1), jnp.where(lower, 2, 1), jnp.where(lower, 3, 0))

    def place(s):
        return pl.ds(pl.multiple_of(planes[s] * n_a, n_a), n_a)

    for s in range(2):
        whole[:, place(s), :] = keep_early[s] + got_early[s]

    @pl.when(middle)
    def _():
        whole[:, place(2), :] = keep_early[2] + got_early[2]
        whole[:, place(3), :] = keep_late[...] + got_late[...]

    @pl.when(jnp.logical_not(middle))
    def _():
        whole[:, place(2), :] = keep_late[...] + got_late[...]
        whole[:, place(3), :] = across[...] + across_other[...]

    n_rows, block_a = virt.shape
    spread = [jnp.broadcast_to(virt[k : k + 1, :], (n_a, block_a)) for k in range(n_rows)]
    lane = lax.broadcasted_iota(jnp.int32, (n_b, block_a), 1)
    place_b = lax.rem(lax.broadcasted_iota(jnp.int32, (n_b, block_a), 0), n_a) + col * n_a
    b_labels = jnp.sum(jnp.where(lane == place_b, jnp.concatenate(spread, axis=0), 0), axis=1, keepdims=True)
    pair_sym = jnp.bitwise_xor(b_labels, virt[pl.ds(row, 1), :])
    first = lax.axis_index("pair") * n_p
    for p in range(n_p):
        out[p] = jnp.where(pair_sym == pair_symmetry(occ, pairs, first + p), whole[p].T, 0.0)


def swap(array, axis, mask):
    size = lax.axis_size(axis)
    return lax.ppermute(array, axis, [(i, i ^ mask) for i in range(size)])


def staged_body(factors, amplitudes, virt_irreps, win_irreps, occ_irreps, pair_list):
    n_fit, per_device, width = factors.shape
    n_rows = lax.axis_size("row")
    n_cols = lax.axis_size("col")
    n_pair = lax.axis_size("pair")
    n_b = n_rows * per_device
    block_a = per_device * n_cols
    slab = amplitudes.shape[0]
    n = per_device * width
    rest = n_fit % LANES
    below = 16 * pl.cdiv(rest * (n // LANES), 16)
    depth = n_fit - rest + LANES

    anywhere = pl.BlockSpec(memory_space=pl.ANY)
    vmem = pl.BlockSpec(memory_space=pltpu.VMEM)
    smem = pl.BlockSpec(memory_space=pltpu.SMEM)
    params = pltpu.CompilerParams(vmem_limit_bytes=VMEM_LIMIT)

    own = pl.pallas_call(
        lambda *refs: pack_kernel(rest, *refs),
        out_shape=jax.ShapeDtypeStruct((n + below, n_fit - rest), jnp.bfloat16),
        in_specs=[vmem],
        out_specs=vmem,
        compiler_params=params,
        name="pack",
    )(jnp.transpose(factors, (1, 2, 0)).reshape(n, n_fit))

    def at(r, c):
        return r * n_cols + c

    facing = swap(own, "col", 1)
    turned = lax.ppermute(
        own,
        ("row", "col"),
        [(at(r, c), at(r, 3 - c) if c in (1, 2) else at(r ^ 2, c)) for r in range(n_rows) for c in range(n_cols)],
    )
    by_x = lax.ppermute(own, ("row", "col"), [(at(r, c), at(r ^ 2, c)) for r in range(n_rows) for c in (1, 2)])
    by_core = swap(own, "row", 1)
    other_amplitudes = swap(amplitudes, "pair", 1)

    far = lax.ppermute(facing, "col", [(1, 2), (2, 1)])
    passed = swap(turned, "col", 1)
    x_rows = jnp.where(is_middle(), by_x, turned)
    by_both = swap(x_rows, "row", 1)

    def middle_core_swap(array):
        return lax.ppermute(array, ("row", "col"), [(at(r, c), at(r ^ 1, c)) for r in range(n_rows) for c in (1, 2)])

    facing_core = middle_core_swap(facing)
    passed_core = middle_core_swap(passed)

    block = jax.ShapeDtypeStruct((slab, per_device, n_b), jnp.float32)
    blocks = jax.ShapeDtypeStruct((3, slab, per_device, n_b), jnp.float32)
    panel_shape = (width, n_rows, per_device, depth)
    panel_scratch = pltpu.VMEM(panel_shape, jnp.bfloat16)
    split_scratch = pltpu.VMEM((per_device, 2, width, width, n_b), jnp.bfloat16)
    n_p = 16 * pl.cdiv(slab, 16)
    sums_scratch = pltpu.VMEM((per_device * 2 * n_p, n_b), jnp.float32)
    pairs = jnp.transpose(pair_list)

    def held(*count):
        return [pltpu.VMEM(count + (n, depth), jnp.bfloat16), pltpu.VMEM(count + (below, LANES), jnp.bfloat16)]

    def cost(n_blocks):
        flops = 2 * n_blocks * n * n_b * width * depth
        return pl.CostEstimate(flops=flops, bytes_accessed=8 * n * depth, transcendentals=0)

    keep_early, send_early, panel, weights = pl.pallas_call(
        lambda *refs: early_kernel(rest, *refs),
        out_shape=(
            blocks,
            blocks,
            jax.ShapeDtypeStruct(panel_shape, jnp.bfloat16),
            jax.ShapeDtypeStruct((2 * n_p, 2 * width * width), jnp.bfloat16),
        ),
        in_specs=[anywhere] * 6 + [vmem] * 2 + [smem] * 3,
        out_specs=(vmem, vmem, anywhere, vmem),
        scratch_shapes=[
            panel_scratch,
            *held(6),
            split_scratch,
            sums_scratch,
            pltpu.SemaphoreType.DMA((6, 2)),
            pltpu.SemaphoreType.DMA,
        ],
        compiler_params=params,
        cost_estimate=cost(3),
        name="early",
    )(
        own, by_core, by_x, by_both, facing, turned,
        amplitudes.reshape(slab * width, width), other_amplitudes.reshape(slab * width, width),
        win_irreps, occ_irreps, pairs,
    )
    got_early = swap(send_early, "pair", 1)

    keep_across, send_across = pl.pallas_call(
        lambda *refs: across_kernel(rest, *refs),
        out_shape=(block, block),
        in_specs=[anywhere] * 5 + [vmem],
        out_specs=(vmem, vmem),
        scratch_shapes=[panel_scratch, *held(5), split_scratch, sums_scratch, pltpu.SemaphoreType.DMA((5, 2))],
        compiler_params=params,
        cost_estimate=cost(1),
        name="across",
    )(far, facing, facing_core, passed, passed_core, weights)
    outwards = [(c, y, 0 if c == 1 else 3) for c in (1, 2) for y in range(n_pair)]
    across = lax.ppermute(keep_across, "col", [(1, 0), (2, 3)])
    across_other = lax.ppermute(
        send_across, ("col", "pair"), [(c * n_pair + y, to * n_pair + (y ^ 1)) for c, y, to in outwards]
    )

    keep_late, send_late = pl.pallas_call(
        lambda *refs: late_kernel(rest, *refs),
        out_shape=(block, block),
        in_specs=[anywhere] * 3 + [vmem],
        out_specs=(vmem, vmem),
        scratch_shapes=[
            panel_scratch,
            *held(),
            split_scratch,
            sums_scratch,
            pltpu.SemaphoreType.DMA((2,)),
            pltpu.SemaphoreType.DMA,
        ],
        compiler_params=params,
        cost_estimate=cost(1),
        name="late",
    )(far, passed, panel, weights)
    got_late = swap(send_late, "pair", 1)

    out = pl.pallas_call(
        finish_kernel,
        out_shape=jax.ShapeDtypeStruct((slab, n_b, block_a), jnp.float32),
        in_specs=[vmem] + [smem] * 2 + [vmem] * 6,
        out_specs=vmem,
        scratch_shapes=[pltpu.VMEM((slab, block_a, n_b), jnp.float32)],
        compiler_params=params,
        name="finish",
    )(
        virt_irreps.reshape(n_rows, block_a), occ_irreps, pairs,
        keep_early, got_early, keep_late, got_late, across, across_other,
    )
    return jnp.transpose(out.reshape(slab, n_rows, per_device, block_a), (0, 3, 1, 2))


def solution(mesh):
    staged = (mesh.shape["row"], mesh.shape["col"], mesh.shape["pair"]) == (4, 4, 2)
    body = staged_body if staged else gathered_body
    in_specs = (P("pair", ("row", "col"), None), P("pair", None, None), P(), P(), P(), P())
    out_specs = P("pair", "row", None, "col")
    return jax.shard_map(body, mesh=mesh, in_specs=in_specs, out_specs=out_specs, check_vma=False)
```

```python
import jax
import jax.numpy as jnp
from jax import lax
from jax.experimental import pallas as pl
from jax.experimental.pallas import tpu as pltpu
from jax.sharding import PartitionSpec as P

VMEM_LIMIT = 24 * 1024 * 1024
LANES = 128
NT = (((1,), (1,)), ((), ()))
NN = (((1,), (0,)), ((), ()))
TN = (((0,), (0,)), ((), ()))


def lookup_symmetry(occ_irreps, pair_list):
    labels = jnp.arange(occ_irreps.shape[0], dtype=jnp.int32)
    onehot = pair_list[:, :, None] == labels[None, None, :]
    picked = jnp.sum(jnp.where(onehot, occ_irreps[None, None, :], 0), axis=-1)
    return jnp.bitwise_xor(picked[:, 0], picked[:, 1])


def mask_amplitudes(amplitudes, win_irreps, symmetry):
    product = jnp.bitwise_xor(win_irreps[:, None], win_irreps[None, :])
    allowed = product[None, :, :] == symmetry[:, None, None]
    return jnp.where(allowed, amplitudes, jnp.zeros_like(amplitudes))


def gathered_body(factors, amplitudes, virt_irreps, win_irreps, occ_irreps, pair_list):
    per_device = factors.shape[1]
    n_rows = lax.axis_size("row")
    n_cols = lax.axis_size("col")
    block_a = per_device * n_cols
    slab = amplitudes.shape[0]
    symmetry = lookup_symmetry(occ_irreps, pair_list)
    own_symmetry = lax.dynamic_slice_in_dim(symmetry, lax.axis_index("pair") * slab, slab)
    every = lax.all_gather(amplitudes, "pair", axis=0, tiled=True)
    weights = mask_amplitudes(every, win_irreps, symmetry).astype(jnp.float32)
    n_fitting, _, width = factors.shape
    b_rows = lax.all_gather(factors, "row", axis=1, tiled=True)
    a_rows = lax.all_gather(factors, "col", axis=1, tiled=True)
    integral = lax.dot_general(
        a_rows.reshape(n_fitting, block_a * width),
        b_rows.reshape(n_fitting, n_rows * per_device * width),
        (((0,), (0,)), ((), ())),
        preferred_element_type=jnp.float32,
    )
    integral = integral.reshape(block_a, width, n_rows * per_device, width)
    part = jnp.einsum("acbd,pcd->pab", integral, weights, precision=lax.Precision.HIGHEST)
    full = lax.psum_scatter(part, "pair", scatter_dimension=0, tiled=True)
    full = full.reshape(slab, block_a, n_rows, per_device)
    a_labels = lax.dynamic_slice_in_dim(virt_irreps, lax.axis_index("row") * block_a, block_a)
    b_labels = lax.dynamic_slice_in_dim(
        virt_irreps.reshape(n_rows, -1), lax.axis_index("col") * per_device, per_device, 1
    )
    pair_sym = jnp.bitwise_xor(a_labels[:, None, None], b_labels[None, :, :])
    allowed = pair_sym[None, :, :, :] == own_symmetry[:, None, None, None]
    return jnp.where(allowed, full, 0.0)


def is_middle():
    col = lax.axis_index("col")
    return jnp.logical_or(col == 1, col == 2)


def one_hot(shape, wanted):
    first = lax.broadcasted_iota(jnp.int32, shape, 0)
    second = lax.broadcasted_iota(jnp.int32, shape, 1)
    return wanted(first, second).astype(jnp.bfloat16)


def multiply(left, right, dims):
    return lax.dot_general(left, right, dims, preferred_element_type=jnp.float32)


def pack_kernel(rest, own, out):
    n, n_fit = own.shape
    whole = n_fit - rest
    out[:n, :] = own[:, :whole]
    below = out.shape[0] - n
    turned = jnp.zeros((below, LANES), jnp.float32)
    for j in range(n // LANES):
        pick = one_hot((below, rest), lambda r, q: r == j * rest + q)
        turned = turned + multiply(pick, own[j * LANES : (j + 1) * LANES, whole:], NT)
    out[n:, :] = jnp.zeros((below, whole), jnp.bfloat16)
    out[n:, :LANES] = turned.astype(jnp.bfloat16)


def fetch(packed, rows, tail, sems):
    n, depth = rows.shape
    whole = depth - LANES
    copies = (
        pltpu.make_async_copy(packed.at[pl.ds(0, n)], rows.at[:, pl.ds(0, whole)], sems.at[0]),
        pltpu.make_async_copy(packed.at[pl.ds(n, tail.shape[0]), pl.ds(0, LANES)], tail, sems.at[1]),
    )
    for copy in copies:
        copy.start()
    return copies


def unpack(copies, rows, tail, rest):
    for copy in copies:
        copy.wait()
    n, depth = rows.shape
    for j in range(n // LANES):
        pick = one_hot(tail.shape, lambda r, q: jnp.logical_and(r == j * rest + q, q < rest))
        back = multiply(tail[...], pick, TN).astype(jnp.bfloat16)
        rows[j * LANES : (j + 1) * LANES, depth - LANES :] = back


def window_major(width, per_device):
    n = width * per_device
    return one_hot((n, n), lambda i, j: lax.rem(i, per_device) * width + lax.div(i, per_device) == j)


def place_rows(panel, order, rows, k):
    width, _, per_device, depth = panel.shape
    moved = multiply(order, rows[...], NN).astype(panel.dtype)
    panel[:, pl.ds(k, 1)] = moved.reshape(width, 1, per_device, depth)


def contract_block(rows, panel, weights, split, sums, keep, send):
    width, n_rows, per_device, depth = panel.shape
    n_b = n_rows * per_device
    n_a = rows.shape[0] // width
    half = keep.shape[0]
    n_p = weights.shape[0]

    def integrals(step, carry):
        two = panel[pl.ds(2 * step, 2)].reshape(2 * n_b, depth)
        acc = multiply(rows[...], two, NT)
        high = acc.astype(jnp.bfloat16)
        low = (acc - high.astype(jnp.float32)).astype(jnp.bfloat16)
        for j in range(2):
            lanes = slice(j * n_b, (j + 1) * n_b)
            split[:, 0, pl.ds(2 * step + j, 1)] = high[:, lanes].reshape(n_a, 1, width, n_b)
            split[:, 1, pl.ds(2 * step + j, 1)] = low[:, lanes].reshape(n_a, 1, width, n_b)
        return carry

    lax.fori_loop(0, width // 2, integrals, 0, unroll=True)

    def ladder(step, carry):
        two = [split[2 * step + j].reshape(2 * width * width, n_b) for j in range(2)]
        res = multiply(weights[...], jnp.concatenate(two, axis=1), NN)
        for j in range(2):
            sums[pl.ds((2 * step + j) * n_p, n_p), :] = res[:, j * n_b : (j + 1) * n_b]
        return carry

    lax.fori_loop(0, n_a // 2, ladder, 0, unroll=True)
    for p in range(half):
        keep[p] = sums[pl.ds(p, n_a, stride=n_p), :]
        send[p] = sums[pl.ds(n_p // 2 + p, n_a, stride=n_p), :]


def pair_symmetry(occ, pairs, p):
    return jnp.bitwise_xor(occ[pairs[0, p]], occ[pairs[1, p]])


def weight_rows(amplitudes, win, occ, pairs, place, n_p):
    width = amplitudes.shape[1]
    n = amplitudes.shape[0]
    slab = n // width
    first = place * slab
    lanes = width * width
    spread = multiply(amplitudes[...], one_hot((width, lanes), lambda d, l: d == lax.div(l, width)), NN)
    c_of_row = lax.rem(lax.broadcasted_iota(jnp.int32, (n, lanes), 0), width)
    c_of_lane = lax.rem(lax.broadcasted_iota(jnp.int32, (n, lanes), 1), width)
    spread = jnp.where(c_of_row == c_of_lane, spread, 0.0).astype(jnp.bfloat16)
    gathered = multiply(one_hot((n_p, n), lambda p, r: p == lax.div(r, width)), spread, NN)
    lane = lax.broadcasted_iota(jnp.int32, (n_p, lanes), 1)
    row = lax.broadcasted_iota(jnp.int32, (n_p, lanes), 0)
    product = jnp.zeros((n_p, lanes), jnp.int32)
    for w in range(width):
        label = win[w]
        product = jnp.bitwise_xor(product, jnp.where(lax.div(lane, width) == w, label, 0))
        product = jnp.bitwise_xor(product, jnp.where(lax.rem(lane, width) == w, label, 0))
    wanted = jnp.full((n_p, lanes), -1, jnp.int32)
    for p in range(slab):
        wanted = jnp.where(row == p, pair_symmetry(occ, pairs, first + p), wanted)
    masked = jnp.where(product == wanted, gathered, 0.0).astype(jnp.bfloat16)
    return jnp.concatenate([masked, masked], axis=1)


def prep_kernel(
    rest, own, by_core, mine, others, win, occ, pairs,
    part, own_rows, weights, held, tail, sems,
):
    copies = [fetch(src, dst, tail.at[i], sems.at[i]) for i, (src, dst) in enumerate(((own, own_rows), (by_core, held)))]
    width, _, per_device, _ = part.shape
    n_p = weights.shape[0] // 2
    pair = lax.axis_index("pair")
    weights[:n_p] = weight_rows(mine, win, occ, pairs, pair, n_p)
    weights[n_p:] = weight_rows(others, win, occ, pairs, 1 - pair, n_p)
    order = window_major(width, per_device)
    for i, rows in enumerate((own_rows, held)):
        unpack(copies[i], rows, tail.at[i], rest)
        place_rows(part, order, rows, i)


def outer_kernel(rest, facing, by_core, part, held, tails, sems):
    @pl.when(is_middle())
    def _():
        width, _, per_device, _ = part.shape
        copies = [fetch(src, held.at[i], tails.at[i], sems.at[i]) for i, src in enumerate((facing, by_core))]
        order = window_major(width, per_device)
        for i in range(2):
            unpack(copies[i], held.at[i], tails.at[i], rest)
            place_rows(part, order, held.at[i], i)


def fetch_part(part, panel, sems):
    row = lax.axis_index("row")
    copies = []
    for i in range(part.shape[1]):
        to = panel.at[:, pl.ds(jnp.bitwise_xor(row, i), 1)]
        copies.append(pltpu.make_async_copy(part.at[:, pl.ds(i, 1)], to, sems.at[i]))
        copies[-1].start()
    return copies


def early_kernel(
    rest, own_rows, part, by_x, by_both, facing, turned, weights,
    keep, send, panel_out, panel, held, tails, split, sums, sems, own_sem, part_sems, panel_sem,
):
    middle = is_middle()
    row = lax.axis_index("row")
    width, _, per_device, _ = panel.shape
    both = fetch(by_both, held.at[1], tails.at[1], sems.at[1])

    @pl.when(middle)
    def _():
        fetch(by_x, held.at[0], tails.at[0], sems.at[0])

    @pl.when(jnp.logical_not(middle))
    def _():
        fetch(turned, held.at[0], tails.at[0], sems.at[0])

    parts = fetch_part(part, panel, part_sems)
    own = pltpu.make_async_copy(own_rows, held.at[2], own_sem)
    own.start()
    copies = [fetch(src, held.at[i], tails.at[i], sems.at[i]) for i, src in ((3, facing), (4, turned))]
    order = window_major(width, per_device)
    for i, waits in enumerate((wait_only(by_x, held.at[0], tails.at[0], sems.at[0]), both)):
        unpack(waits, held.at[i], tails.at[i], rest)
        place_rows(panel, order, held.at[i], jnp.bitwise_xor(row, 2 + i))
    for copy in parts:
        copy.wait()
    back = pltpu.make_async_copy(panel, panel_out, panel_sem)
    back.start()
    own.wait()
    for i, waits in enumerate(copies):
        unpack(waits, held.at[3 + i], tails.at[3 + i], rest)

    def block(s, carry):
        contract_block(held.at[2 + s], panel, weights, split, sums, keep.at[s], send.at[s])
        return carry

    lax.fori_loop(0, jnp.where(middle, 3, 2), block, 0)
    back.wait()


def wait_only(packed, rows, tail, sems):
    n, depth = rows.shape
    return (
        pltpu.make_async_copy(packed.at[pl.ds(0, n)], rows.at[:, pl.ds(0, depth - LANES)], sems.at[0]),
        pltpu.make_async_copy(packed.at[pl.ds(n, tail.shape[0]), pl.ds(0, LANES)], tail, sems.at[1]),
    )


def across_kernel(
    rest, far, part, by_x, by_both, weights, keep, send, panel, held, tails, split, sums, sems, part_sems
):
    @pl.when(is_middle())
    def _():
        copies = [fetch(src, held.at[i], tails.at[i], sems.at[i]) for i, src in enumerate((by_x, by_both, far))]
        parts = fetch_part(part, panel, part_sems)
        width, _, per_device, _ = panel.shape
        row = lax.axis_index("row")
        order = window_major(width, per_device)
        for i in range(2):
            unpack(copies[i], held.at[i], tails.at[i], rest)
            place_rows(panel, order, held.at[i], jnp.bitwise_xor(row, 2 + i))
        unpack(copies[2], held.at[2], tails.at[2], rest)
        for copy in parts:
            copy.wait()
        contract_block(held.at[2], panel, weights, split, sums, keep, send)


def late_kernel(rest, far, passed, panel_in, weights, keep, send, panel, held, tail, split, sums, sems, panel_sem):
    copy_panel = pltpu.make_async_copy(panel_in, panel, panel_sem)
    copy_panel.start()
    middle = is_middle()

    @pl.when(middle)
    def _():
        fetch(far, held, tail, sems)

    @pl.when(jnp.logical_not(middle))
    def _():
        fetch(passed, held, tail, sems)

    unpack(wait_only(far, held, tail, sems), held, tail, rest)
    copy_panel.wait()
    contract_block(held, panel, weights, split, sums, keep, send)


def finish_kernel(
    virt, occ, pairs, keep_early, got_early, keep_late, got_late, across, across_other, out, whole
):
    row = lax.axis_index("row")
    col = lax.axis_index("col")
    middle = is_middle()
    lower = col < 2
    n_p, n_a, n_b = keep_late.shape
    planes = (col, jnp.bitwise_xor(col, 1), jnp.where(lower, 2, 1), jnp.where(lower, 3, 0))

    def place(s):
        return pl.ds(pl.multiple_of(planes[s] * n_a, n_a), n_a)

    for s in range(2):
        whole[:, place(s), :] = keep_early[s] + got_early[s]

    @pl.when(middle)
    def _():
        whole[:, place(2), :] = keep_early[2] + got_early[2]
        whole[:, place(3), :] = keep_late[...] + got_late[...]

    @pl.when(jnp.logical_not(middle))
    def _():
        whole[:, place(2), :] = keep_late[...] + got_late[...]
        whole[:, place(3), :] = across[...] + across_other[...]

    n_rows, block_a = virt.shape
    spread = [jnp.broadcast_to(virt[k : k + 1, :], (n_a, block_a)) for k in range(n_rows)]
    lane = lax.broadcasted_iota(jnp.int32, (n_b, block_a), 1)
    place_b = lax.rem(lax.broadcasted_iota(jnp.int32, (n_b, block_a), 0), n_a) + col * n_a
    b_labels = jnp.sum(jnp.where(lane == place_b, jnp.concatenate(spread, axis=0), 0), axis=1, keepdims=True)
    pair_sym = jnp.bitwise_xor(b_labels, virt[pl.ds(row, 1), :])
    first = lax.axis_index("pair") * n_p
    for p in range(n_p):
        out[p] = jnp.where(pair_sym == pair_symmetry(occ, pairs, first + p), whole[p].T, 0.0)


def swap(array, axis, mask):
    size = lax.axis_size(axis)
    return lax.ppermute(array, axis, [(i, i ^ mask) for i in range(size)])


def staged_body(factors, amplitudes, virt_irreps, win_irreps, occ_irreps, pair_list):
    n_fit, per_device, width = factors.shape
    n_rows = lax.axis_size("row")
    n_cols = lax.axis_size("col")
    n_pair = lax.axis_size("pair")
    n_b = n_rows * per_device
    block_a = per_device * n_cols
    slab = amplitudes.shape[0]
    n = per_device * width
    rest = n_fit % LANES
    below = 16 * pl.cdiv(rest * (n // LANES), 16)
    depth = n_fit - rest + LANES

    anywhere = pl.BlockSpec(memory_space=pl.ANY)
    vmem = pl.BlockSpec(memory_space=pltpu.VMEM)
    smem = pl.BlockSpec(memory_space=pltpu.SMEM)
    params = pltpu.CompilerParams(vmem_limit_bytes=VMEM_LIMIT)

    own = pl.pallas_call(
        lambda *refs: pack_kernel(rest, *refs),
        out_shape=jax.ShapeDtypeStruct((n + below, n_fit - rest), jnp.bfloat16),
        in_specs=[vmem],
        out_specs=vmem,
        compiler_params=params,
        name="pack",
    )(jnp.transpose(factors, (1, 2, 0)).reshape(n, n_fit))

    def at(r, c):
        return r * n_cols + c

    block = jax.ShapeDtypeStruct((slab, per_device, n_b), jnp.float32)
    blocks = jax.ShapeDtypeStruct((3, slab, per_device, n_b), jnp.float32)
    n_p = 16 * pl.cdiv(slab, 16)
    split_scratch = pltpu.VMEM((per_device, 2, width, width, n_b), jnp.bfloat16)
    sums_scratch = pltpu.VMEM((per_device * 2 * n_p, n_b), jnp.float32)
    pairs = jnp.transpose(pair_list)

    def panel(count):
        return jax.ShapeDtypeStruct((width, count, per_device, depth), jnp.bfloat16)

    panel_scratch = pltpu.VMEM(panel(n_rows).shape, jnp.bfloat16)

    def held(*count):
        return [pltpu.VMEM(count + (n, depth), jnp.bfloat16), pltpu.VMEM(count + (below, LANES), jnp.bfloat16)]

    def sems(*count):
        return pltpu.SemaphoreType.DMA(count)

    def cost(n_blocks):
        flops = 20 * n_blocks * n * n_b * width * depth
        return pl.CostEstimate(flops=flops, bytes_accessed=8 * n * depth, transcendentals=0)

    facing = swap(own, "col", 1)
    turned = lax.ppermute(
        own,
        ("row", "col"),
        [(at(r, c), at(r, 3 - c) if c in (1, 2) else at(r ^ 2, c)) for r in range(n_rows) for c in range(n_cols)],
    )
    by_x = lax.ppermute(
        own,
        ("row", "col"),
        [(at(r, c), at(r ^ 2 if c in (1, 2) else r ^ 1, c)) for r in range(n_rows) for c in range(n_cols)],
    )
    by_core = swap(own, "row", 1)
    others = swap(amplitudes, "pair", 1)

    own_part, own_rows, weights = pl.pallas_call(
        lambda *refs: prep_kernel(rest, *refs),
        out_shape=(
            panel(2),
            jax.ShapeDtypeStruct((n, depth), jnp.bfloat16),
            jax.ShapeDtypeStruct((2 * n_p, 2 * width * width), jnp.bfloat16),
        ),
        in_specs=[anywhere] * 2 + [vmem] * 2 + [smem] * 3,
        out_specs=(vmem, vmem, vmem),
        scratch_shapes=[
            pltpu.VMEM((n, depth), jnp.bfloat16), pltpu.VMEM((2, below, LANES), jnp.bfloat16), sems(2, 2)
        ],
        compiler_params=params,
        cost_estimate=cost(1),
        name="prep",
    )(
        own, by_core,
        amplitudes.reshape(slab * width, width), others.reshape(slab * width, width), win_irreps, occ_irreps, pairs,
    )

    def middle_or_core(array):
        pairs = [(at(r, c), at(r, 3 - c) if c in (1, 2) else at(r ^ 1, c)) for r in range(n_rows) for c in range(n_cols)]
        return lax.ppermute(array, ("row", "col"), pairs)

    far = middle_or_core(facing)
    passed = swap(turned, "col", 1)
    x_rows = jnp.where(is_middle(), by_x, turned)
    by_both = swap(x_rows, "row", 1)

    facing_core = swap(facing, "row", 1)

    keep_early, send_early, own_panel = pl.pallas_call(
        lambda *refs: early_kernel(rest, *refs),
        out_shape=(blocks, blocks, panel(n_rows)),
        in_specs=[anywhere] * 6 + [vmem],
        out_specs=(vmem, vmem, anywhere),
        scratch_shapes=[
            panel_scratch, *held(5), split_scratch, sums_scratch, sems(5, 2), sems(), sems(2), sems()
        ],
        compiler_params=params,
        cost_estimate=cost(3),
        name="early",
    )(own_rows, own_part, by_x, by_both, facing, turned, weights)
    got_early = swap(send_early, "pair", 1)

    outer_part = pl.pallas_call(
        lambda *refs: outer_kernel(rest, *refs),
        out_shape=panel(2),
        in_specs=[anywhere] * 2,
        out_specs=vmem,
        scratch_shapes=[*held(2), sems(2, 2)],
        compiler_params=params,
        cost_estimate=cost(1),
        name="outer",
    )(facing, facing_core)

    passed, _, _ = lax.optimization_barrier((passed, own_panel, outer_part))
    passed_core = swap(passed, "row", 1)
    keep_late, send_late = pl.pallas_call(
        lambda *refs: late_kernel(rest, *refs),
        out_shape=(block, block),
        in_specs=[anywhere] * 3 + [vmem],
        out_specs=(vmem, vmem),
        scratch_shapes=[panel_scratch, *held(), split_scratch, sums_scratch, sems(2), sems()],
        compiler_params=params,
        cost_estimate=cost(1),
        name="late",
    )(far, passed, own_panel, weights)

    passed_core, _ = lax.optimization_barrier((passed_core, keep_late))
    keep_across, send_across = pl.pallas_call(
        lambda *refs: across_kernel(rest, *refs),
        out_shape=(block, block),
        in_specs=[anywhere] * 4 + [vmem],
        out_specs=(vmem, vmem),
        scratch_shapes=[panel_scratch, *held(3), split_scratch, sums_scratch, sems(3, 2), sems(2)],
        compiler_params=params,
        cost_estimate=cost(1),
        name="across",
    )(far, outer_part, passed, passed_core, weights)
    across = swap(keep_across, "col", 1)
    across_other = lax.ppermute(
        send_across,
        ("col", "pair"),
        [(c * n_pair + y, (c ^ 1) * n_pair + (y ^ 1)) for c in range(n_cols) for y in range(n_pair)],
    )
    got_late = swap(lax.optimization_barrier((send_late, keep_across))[0], "pair", 1)

    out = pl.pallas_call(
        finish_kernel,
        out_shape=jax.ShapeDtypeStruct((slab, n_b, block_a), jnp.float32),
        in_specs=[vmem] + [smem] * 2 + [vmem] * 6,
        out_specs=vmem,
        scratch_shapes=[pltpu.VMEM((slab, block_a, n_b), jnp.float32)],
        compiler_params=params,
        name="finish",
    )(
        virt_irreps.reshape(n_rows, block_a), occ_irreps, pairs,
        keep_early, got_early, keep_late, got_late, across, across_other,
    )
    return jnp.transpose(out.reshape(slab, n_rows, per_device, block_a), (0, 3, 1, 2))


def solution(mesh):
    staged = (mesh.shape["row"], mesh.shape["col"], mesh.shape["pair"]) == (4, 4, 2)
    body = staged_body if staged else gathered_body
    in_specs = (P("pair", ("row", "col"), None), P("pair", None, None), P(), P(), P(), P())
    out_specs = P("pair", "row", None, "col")
    return jax.shard_map(body, mesh=mesh, in_specs=in_specs, out_specs=out_specs, check_vma=False)
```

```python
import jax
import jax.numpy as jnp
from jax import lax
from jax.experimental import pallas as pl
from jax.experimental.pallas import tpu as pltpu
from jax.sharding import PartitionSpec as P

VMEM_LIMIT = 24 * 1024 * 1024
LANES = 128
NT = (((1,), (1,)), ((), ()))
NN = (((1,), (0,)), ((), ()))
TN = (((0,), (0,)), ((), ()))


def lookup_symmetry(occ_irreps, pair_list):
    labels = jnp.arange(occ_irreps.shape[0], dtype=jnp.int32)
    onehot = pair_list[:, :, None] == labels[None, None, :]
    picked = jnp.sum(jnp.where(onehot, occ_irreps[None, None, :], 0), axis=-1)
    return jnp.bitwise_xor(picked[:, 0], picked[:, 1])


def mask_amplitudes(amplitudes, win_irreps, symmetry):
    product = jnp.bitwise_xor(win_irreps[:, None], win_irreps[None, :])
    allowed = product[None, :, :] == symmetry[:, None, None]
    return jnp.where(allowed, amplitudes, jnp.zeros_like(amplitudes))


def gathered_body(factors, amplitudes, virt_irreps, win_irreps, occ_irreps, pair_list):
    per_device = factors.shape[1]
    n_rows = lax.axis_size("row")
    n_cols = lax.axis_size("col")
    block_a = per_device * n_cols
    slab = amplitudes.shape[0]
    symmetry = lookup_symmetry(occ_irreps, pair_list)
    own_symmetry = lax.dynamic_slice_in_dim(symmetry, lax.axis_index("pair") * slab, slab)
    every = lax.all_gather(amplitudes, "pair", axis=0, tiled=True)
    weights = mask_amplitudes(every, win_irreps, symmetry).astype(jnp.float32)
    n_fitting, _, width = factors.shape
    b_rows = lax.all_gather(factors, "row", axis=1, tiled=True)
    a_rows = lax.all_gather(factors, "col", axis=1, tiled=True)
    integral = lax.dot_general(
        a_rows.reshape(n_fitting, block_a * width),
        b_rows.reshape(n_fitting, n_rows * per_device * width),
        (((0,), (0,)), ((), ())),
        preferred_element_type=jnp.float32,
    )
    integral = integral.reshape(block_a, width, n_rows * per_device, width)
    part = jnp.einsum("acbd,pcd->pab", integral, weights, precision=lax.Precision.HIGHEST)
    full = lax.psum_scatter(part, "pair", scatter_dimension=0, tiled=True)
    full = full.reshape(slab, block_a, n_rows, per_device)
    a_labels = lax.dynamic_slice_in_dim(virt_irreps, lax.axis_index("row") * block_a, block_a)
    b_labels = lax.dynamic_slice_in_dim(
        virt_irreps.reshape(n_rows, -1), lax.axis_index("col") * per_device, per_device, 1
    )
    pair_sym = jnp.bitwise_xor(a_labels[:, None, None], b_labels[None, :, :])
    allowed = pair_sym[None, :, :, :] == own_symmetry[:, None, None, None]
    return jnp.where(allowed, full, 0.0)


def is_middle():
    col = lax.axis_index("col")
    return jnp.logical_or(col == 1, col == 2)


def one_hot(shape, wanted):
    first = lax.broadcasted_iota(jnp.int32, shape, 0)
    second = lax.broadcasted_iota(jnp.int32, shape, 1)
    return wanted(first, second).astype(jnp.bfloat16)


def multiply(left, right, dims):
    return lax.dot_general(left, right, dims, preferred_element_type=jnp.float32)


def pack_kernel(rest, own, out):
    n, n_fit = own.shape
    whole = n_fit - rest
    below = out.shape[0] - n
    turned = jnp.zeros((below, LANES), jnp.float32)
    for j in range(n // LANES):
        pick = one_hot((below, rest), lambda r, q: r == j * rest + q)
        turned = turned + multiply(pick, own[j * LANES : (j + 1) * LANES, whole:], NT)
    out[:n, :] = own[:, :whole]
    out[n:, :] = jnp.zeros((below, whole), jnp.bfloat16)
    out[n:, :LANES] = turned.astype(jnp.bfloat16)


class Rows:
    def __init__(self, packed, rows, tail, sems, rest, start=0):
        n, depth = rows.shape
        below = tail.shape[0]
        all_rows = packed.shape[0] - below
        self.copies = (
            pltpu.make_async_copy(packed.at[pl.ds(start, n)], rows.at[:, pl.ds(0, depth - LANES)], sems.at[0]),
            pltpu.make_async_copy(packed.at[pl.ds(all_rows, below), pl.ds(0, LANES)], tail, sems.at[1]),
        )
        self.rows, self.tail, self.rest, self.segment = rows, tail, rest, start // LANES

    def start(self):
        for copy in self.copies:
            copy.start()
        return self

    def ready(self):
        for copy in self.copies:
            copy.wait()
        rows, tail, rest = self.rows, self.tail, self.rest
        n, depth = rows.shape
        for j in range(n // LANES):
            base = (self.segment + j) * rest
            pick = one_hot(tail.shape, lambda r, q: jnp.logical_and(r == base + q, q < rest))
            back = multiply(tail[...], pick, TN).astype(jnp.bfloat16)
            rows[j * LANES : (j + 1) * LANES, depth - LANES :] = back
        return rows


def window_major(width, per_device):
    n = width * per_device
    into = lax.broadcasted_iota(jnp.int32, (n, 1), 0)
    wanted = lax.rem(into, per_device) * width + lax.div(into, per_device)
    return (lax.broadcasted_iota(jnp.int32, (n, n), 1) == wanted).astype(jnp.bfloat16)


def place_rows(panel, order, rows, k):
    width, _, per_device, depth = panel.shape
    half = per_device // 2
    for h in range(2):
        moved = multiply(order, rows[h * half * width : (h + 1) * half * width, :], NN).astype(panel.dtype)
        panel[:, pl.ds(k, 1), h * half : (h + 1) * half] = moved.reshape(width, 1, half, depth)


def contract_block(rows, panel, weights, split, sums, keep, send, to=0):
    width, n_rows, per_device, depth = panel.shape
    n_b = n_rows * per_device
    n_a = rows.shape[0] // width
    slab = keep.shape[0]
    n_p = weights.shape[0]

    def integrals(step, carry):
        two = panel[pl.ds(2 * step, 2)].reshape(2 * n_b, depth)
        acc = multiply(rows[...], two, NT)
        high = acc.astype(jnp.bfloat16)
        low = (acc - high.astype(jnp.float32)).astype(jnp.bfloat16)
        for j in range(2):
            lanes = slice(j * n_b, (j + 1) * n_b)
            split[:n_a, 0, pl.ds(2 * step + j, 1)] = high[:, lanes].reshape(n_a, 1, width, n_b)
            split[:n_a, 1, pl.ds(2 * step + j, 1)] = low[:, lanes].reshape(n_a, 1, width, n_b)
        return carry

    lax.fori_loop(0, width // 2, integrals, 0, unroll=True)

    def ladder(step, carry):
        two = [split[2 * step + j].reshape(2 * width * width, n_b) for j in range(2)]
        res = multiply(weights[...], jnp.concatenate(two, axis=1), NN)
        for j in range(2):
            sums[pl.ds((2 * step + j) * n_p, n_p), :] = res[:, j * n_b : (j + 1) * n_b]
        return carry

    lax.fori_loop(0, n_a // 2, ladder, 0, unroll=True)
    for p in range(slab):
        keep[p, to : to + n_a] = sums[pl.ds(p, n_a, stride=n_p), :]
        send[p, to : to + n_a] = sums[pl.ds(n_p // 2 + p, n_a, stride=n_p), :]


def pair_symmetry(occ, pairs, p):
    return jnp.bitwise_xor(occ[pairs[0, p]], occ[pairs[1, p]])


def weight_rows(amplitudes, win, occ, pairs, place, n_p):
    width = amplitudes.shape[1]
    n = amplitudes.shape[0]
    slab = n // width
    first = place * slab
    lanes = width * width
    spread = multiply(amplitudes[...], one_hot((width, lanes), lambda d, l: d == lax.div(l, width)), NN)
    c_of_row = lax.rem(lax.broadcasted_iota(jnp.int32, (n, lanes), 0), width)
    c_of_lane = lax.rem(lax.broadcasted_iota(jnp.int32, (n, lanes), 1), width)
    spread = jnp.where(c_of_row == c_of_lane, spread, 0.0).astype(jnp.bfloat16)
    gathered = multiply(one_hot((n_p, n), lambda p, r: p == lax.div(r, width)), spread, NN)
    lane = lax.broadcasted_iota(jnp.int32, (n_p, lanes), 1)
    row = lax.broadcasted_iota(jnp.int32, (n_p, lanes), 0)
    product = jnp.zeros((n_p, lanes), jnp.int32)
    for w in range(width):
        label = win[w]
        product = jnp.bitwise_xor(product, jnp.where(lax.div(lane, width) == w, label, 0))
        product = jnp.bitwise_xor(product, jnp.where(lax.rem(lane, width) == w, label, 0))
    wanted = jnp.full((n_p, lanes), -1, jnp.int32)
    for p in range(slab):
        wanted = jnp.where(row == p, pair_symmetry(occ, pairs, first + p), wanted)
    masked = jnp.where(product == wanted, gathered, 0.0).astype(jnp.bfloat16)
    return jnp.concatenate([masked, masked], axis=1)


def prep_kernel(rest, own, by_core, mine, others, win, occ, pairs, part, own_rows, weights, held, tails, sems):
    fetched = [
        Rows(src, dst, tails.at[i], sems.at[i], rest).start() for i, (src, dst) in enumerate(((own, own_rows), (by_core, held)))
    ]
    width, _, per_device, _ = part.shape
    n_p = weights.shape[0] // 2
    pair = lax.axis_index("pair")
    weights[:n_p] = weight_rows(mine, win, occ, pairs, pair, n_p)
    weights[n_p:] = weight_rows(others, win, occ, pairs, 1 - pair, n_p)
    order = window_major(width, per_device // 2)
    for i in range(2):
        place_rows(part, order, fetched[i].ready(), i)


def outer_kernel(rest, facing, by_core, by_x, part, held, tails, sems):
    @pl.when(is_middle())
    def _():
        width, _, per_device, _ = part.shape
        fetched = [Rows(src, held.at[i], tails.at[i], sems.at[i], rest).start() for i, src in enumerate((facing, by_core, by_x))]
        order = window_major(width, per_device // 2)
        for i in range(3):
            place_rows(part, order, fetched[i].ready(), i)


def fetch_part(part, panel, sems):
    row = lax.axis_index("row")
    copies = []
    for i in range(part.shape[1]):
        to = panel.at[:, pl.ds(jnp.bitwise_xor(row, i), 1)]
        copies.append(pltpu.make_async_copy(part.at[:, pl.ds(i, 1)], to, sems.at[i]))
        copies[-1].start()
    return copies


def early_kernel(
    rest, own_rows, part, by_x, by_both, facing, turned, weights,
    keep, send, panel_out, panel, held, tails, split, sums, sems, own_sem, part_sems, panel_sem,
):
    middle = is_middle()
    row = lax.axis_index("row")
    width, _, per_device, _ = panel.shape
    x_rows = Rows(by_x, held.at[0], tails.at[0], sems.at[0], rest)
    both = Rows(by_both, held.at[1], tails.at[1], sems.at[1], rest).start()

    @pl.when(middle)
    def _():
        x_rows.start()

    @pl.when(jnp.logical_not(middle))
    def _():
        Rows(turned, held.at[0], tails.at[0], sems.at[0], rest).start()

    parts = fetch_part(part, panel, part_sems)
    own = pltpu.make_async_copy(own_rows, held.at[2], own_sem)
    own.start()
    facing_rows = Rows(facing, held.at[3], tails.at[3], sems.at[3], rest).start()
    order = window_major(width, per_device // 2)
    for i, rows in enumerate((x_rows, both)):
        place_rows(panel, order, rows.ready(), jnp.bitwise_xor(row, 2 + i))
    for copy in parts:
        copy.wait()
    back = pltpu.make_async_copy(panel, panel_out, panel_sem)
    back.start()
    own.wait()
    facing_rows.ready()

    def block(s, carry):
        contract_block(held.at[2 + s], panel, weights, split, sums, keep.at[s], send.at[s])
        return carry

    lax.fori_loop(0, 2, block, 0)
    back.wait()


def middle_kernel(rest, turned, panel_in, weights, keep, send, panel, held, tail, split, sums, sems, panel_sem):
    @pl.when(is_middle())
    def _():
        copy_panel = pltpu.make_async_copy(panel_in, panel, panel_sem)
        copy_panel.start()
        Rows(turned, held, tail, sems, rest).start().ready()
        copy_panel.wait()
        contract_block(held, panel, weights, split, sums, keep, send)


def late_kernel(
    rest, far, passed, panel_in, weights, keep, send, panel, held, tail, split, sums, sems, panel_sem
):
    copy_panel = pltpu.make_async_copy(panel_in, panel, panel_sem)
    copy_panel.start()
    middle = is_middle()
    rows = Rows(far, held, tail, sems, rest)

    @pl.when(middle)
    def _():
        rows.start()

    @pl.when(jnp.logical_not(middle))
    def _():
        Rows(passed, held, tail, sems, rest).start()

    rows.ready()
    copy_panel.wait()
    contract_block(held, panel, weights, split, sums, keep, send)


def across_kernel(
    rest, far, part, by_both, weights, keep, send, panel, held, tails, split, sums, sems, part_sems
):
    @pl.when(is_middle())
    def _():
        fetched = [Rows(src, held.at[i], tails.at[i], sems.at[i], rest).start() for i, src in enumerate((by_both, far))]
        parts = fetch_part(part, panel, part_sems)
        width, _, per_device, _ = panel.shape
        row = lax.axis_index("row")
        place_rows(panel, window_major(width, per_device // 2), fetched[0].ready(), jnp.bitwise_xor(row, 3))
        rows = fetched[1].ready()
        for copy in parts:
            copy.wait()
        contract_block(rows, panel, weights, split, sums, keep, send)


def add_kernel(first, second, out):
    out[...] = first[...] + second[...]


def finish_kernel(
    virt, occ, pairs, keep_early, got_early, keep_middle, got_middle, keep_late, got_late,
    across, out, whole,
):
    row = lax.axis_index("row")
    col = lax.axis_index("col")
    middle = is_middle()
    lower = col < 2
    n_p, n_a, n_b = keep_late.shape
    planes = (col, jnp.bitwise_xor(col, 1), jnp.where(lower, 2, 1), jnp.where(lower, 3, 0))

    def place(s):
        return pl.ds(pl.multiple_of(planes[s] * n_a, n_a), n_a)

    for s in range(2):
        whole[:, place(s), :] = keep_early[s] + got_early[s]

    @pl.when(middle)
    def _():
        whole[:, place(2), :] = keep_middle[...] + got_middle[...]
        whole[:, place(3), :] = keep_late[...] + got_late[...]

    @pl.when(jnp.logical_not(middle))
    def _():
        whole[:, place(2), :] = keep_late[...] + got_late[...]
        whole[:, place(3), :] = across[...]

    n_rows, block_a = virt.shape
    spread = [jnp.broadcast_to(virt[k : k + 1, :], (n_a, block_a)) for k in range(n_rows)]
    lane = lax.broadcasted_iota(jnp.int32, (n_b, block_a), 1)
    place_b = lax.rem(lax.broadcasted_iota(jnp.int32, (n_b, block_a), 0), n_a) + col * n_a
    b_labels = jnp.sum(jnp.where(lane == place_b, jnp.concatenate(spread, axis=0), 0), axis=1, keepdims=True)
    pair_sym = jnp.bitwise_xor(b_labels, virt[pl.ds(row, 1), :])
    first = lax.axis_index("pair") * n_p
    for p in range(n_p):
        out[p] = jnp.where(pair_sym == pair_symmetry(occ, pairs, first + p), whole[p].T, 0.0)


def swap(array, axis, mask):
    size = lax.axis_size(axis)
    return lax.ppermute(array, axis, [(i, i ^ mask) for i in range(size)])


def staged_body(factors, amplitudes, virt_irreps, win_irreps, occ_irreps, pair_list):
    n_fit, per_device, width = factors.shape
    n_rows = lax.axis_size("row")
    n_cols = lax.axis_size("col")
    n_pair = lax.axis_size("pair")
    n_b = n_rows * per_device
    block_a = per_device * n_cols
    slab = amplitudes.shape[0]
    n = per_device * width
    half = n // 2
    rest = n_fit % LANES
    below = 16 * pl.cdiv(rest * (n // LANES), 16)
    depth = n_fit - rest + LANES
    n_p = 16 * pl.cdiv(slab, 16)

    anywhere = pl.BlockSpec(memory_space=pl.ANY)
    vmem = pl.BlockSpec(memory_space=pltpu.VMEM)
    smem = pl.BlockSpec(memory_space=pltpu.SMEM)

    def array(*shape, dtype=jnp.bfloat16):
        return jax.ShapeDtypeStruct(shape, dtype)

    def sums_of(*shape):
        return array(*shape, n_b, dtype=jnp.float32)

    def panel(count):
        return array(width, count, per_device, depth)

    def sems(*count):
        return pltpu.SemaphoreType.DMA(count)

    def rows(*shape):
        return pltpu.VMEM(shape + (depth,), jnp.bfloat16)

    def tails(*count):
        return pltpu.VMEM(count + (below, LANES), jnp.bfloat16)

    panel_scratch = pltpu.VMEM(panel(n_rows).shape, jnp.bfloat16)
    work = [
        pltpu.VMEM((per_device, 2, width, width, n_b), jnp.bfloat16),
        pltpu.VMEM((per_device * 2 * n_p, n_b), jnp.float32),
    ]

    def call(kernel, name, out_shape, in_specs, out_specs, scratch, n_blocks=None):
        estimate = None
        if n_blocks is not None:
            flops = int(20 * n_blocks * n * n_b * width * depth)
            estimate = pl.CostEstimate(flops=flops, bytes_accessed=8 * n * depth, transcendentals=0)
        return pl.pallas_call(
            kernel,
            out_shape=out_shape,
            in_specs=in_specs,
            out_specs=out_specs,
            scratch_shapes=scratch,
            compiler_params=pltpu.CompilerParams(vmem_limit_bytes=VMEM_LIMIT),
            cost_estimate=estimate,
            name=name,
        )

    def permute(x, to):
        pairs = [
            (r * n_cols + c, to_r * n_cols + to_c)
            for r in range(n_rows)
            for c in range(n_cols)
            for to_r, to_c in [to(r, c, c in (1, 2))]
        ]
        return lax.ppermute(x, ("row", "col"), pairs)

    def face(x):
        return permute(x, lambda r, c, middle: (r, c ^ 1))

    def turn(x):
        return permute(x, lambda r, c, middle: (r, 3 - c) if middle else (r ^ 2, c))

    def cross(x):
        return permute(x, lambda r, c, middle: (r, 3 - c) if middle else (r ^ 1, c))

    def along_x(x):
        return permute(x, lambda r, c, middle: (r ^ 2, c) if middle else (r ^ 1, c))

    def along_x_to_core(x):
        return permute(x, lambda r, c, middle: (r ^ 3, c) if middle else (r ^ 1, c))

    def core(x):
        return permute(x, lambda r, c, middle: (r ^ 1, c))

    def after(x, *others):
        return lax.optimization_barrier((x, *others))[0]

    own = call(
        lambda *refs: pack_kernel(rest, *refs), "pack", array(n + below, n_fit - rest), [vmem], vmem, []
    )(jnp.transpose(factors, (1, 2, 0)).reshape(n, n_fit))

    turned = turn(own)
    facing = face(own)
    by_x = along_x(own)
    by_core = core(own)
    others = swap(amplitudes, "pair", 1)

    pairs = jnp.transpose(pair_list)
    own_part, own_rows, weights = call(
        lambda *refs: prep_kernel(rest, *refs),
        "prep",
        (panel(2), array(n, depth), array(2 * n_p, 2 * width * width)),
        [anywhere] * 2 + [vmem] * 2 + [smem] * 3,
        (vmem,) * 3,
        [rows(n), tails(2), sems(2, 2)],
        1,
    )(
        own, by_core,
        amplitudes.reshape(slab * width, width), others.reshape(slab * width, width),
        win_irreps, occ_irreps, pairs,
    )

    passed = face(turned)
    far = cross(facing)
    facing_both = along_x_to_core(facing)
    x_rows = jnp.where(is_middle(), by_x, turned)
    by_both = core(x_rows)
    facing_core = core(facing)

    early = sums_of(2, slab, per_device)
    keep_early, send_early, own_panel = call(
        lambda *refs: early_kernel(rest, *refs),
        "early",
        (early, early, panel(n_rows)),
        [anywhere] * 6 + [vmem],
        (vmem, vmem, anywhere),
        [panel_scratch, rows(4, n), tails(4), *work, sems(4, 2), sems(), sems(2), sems()],
        2,
    )(own_rows, own_part, by_x, by_both, facing, turned, weights)
    got_early = swap(send_early, "pair", 1)

    late = sums_of(slab, per_device)
    keep_middle, send_middle = call(
        lambda *refs: middle_kernel(rest, *refs),
        "middle",
        (late, late),
        [anywhere] * 2 + [vmem],
        (vmem, vmem),
        [panel_scratch, rows(n), tails(), *work, sems(2), sems()],
        1,
    )(turned, own_panel, weights)
    got_middle = swap(send_middle, "pair", 1)
    outer_part = call(
        lambda *refs: outer_kernel(rest, *refs),
        "outer",
        panel(3),
        [anywhere] * 3,
        vmem,
        [rows(3, n), tails(3), sems(3, 2)],
        1,
    )(facing, after(facing_core, keep_middle), passed)
    keep_across, send_across = call(
        lambda *refs: across_kernel(rest, *refs),
        "across",
        (late, late),
        [anywhere] * 3 + [vmem],
        (vmem, vmem),
        [panel_scratch, rows(2, n), tails(2), *work, sems(2, 2), sems(3)],
        1,
    )(far, after(outer_part, got_early), facing_both, weights)
    got_across = swap(send_across, "pair", 1)
    keep_late, send_late = call(
        lambda *refs: late_kernel(rest, *refs),
        "late",
        (late, late),
        [anywhere] * 3 + [vmem],
        (vmem, vmem),
        [panel_scratch, rows(n), tails(), *work, sems(2), sems()],
        1,
    )(far, passed, after(own_panel, keep_across, got_middle), weights)
    got_late = swap(send_late, "pair", 1)

    across = face(call(add_kernel, "add", late, [vmem] * 2, vmem, [])(keep_across, got_across))

    out = call(
        finish_kernel,
        "finish",
        sums_of(slab, block_a),
        [vmem] + [smem] * 2 + [vmem] * 7,
        vmem,
        [pltpu.VMEM((slab, block_a, n_b), jnp.float32)],
    )(
        virt_irreps.reshape(n_rows, block_a), occ_irreps, pairs,
        keep_early, got_early, keep_middle, got_middle, keep_late, got_late, across,
    )
    return jnp.transpose(out.reshape(slab, n_rows, per_device, block_a), (0, 3, 1, 2))


def solution(mesh):
    staged = (mesh.shape["row"], mesh.shape["col"], mesh.shape["pair"]) == (4, 4, 2)
    body = staged_body if staged else gathered_body
    in_specs = (P("pair", ("row", "col"), None), P("pair", None, None), P(), P(), P(), P())
    out_specs = P("pair", "row", None, "col")
    return jax.shard_map(body, mesh=mesh, in_specs=in_specs, out_specs=out_specs, check_vma=False)
```

```python
import jax
import jax.numpy as jnp
from jax import lax
from jax.experimental import pallas as pl
from jax.experimental.pallas import tpu as pltpu
from jax.sharding import PartitionSpec as P

VMEM_LIMIT = 16 * 1024 * 1024
LANES = 128
NT = (((1,), (1,)), ((), ()))
NN = (((1,), (0,)), ((), ()))
TN = (((0,), (0,)), ((), ()))


def lookup_symmetry(occ_irreps, pair_list):
    labels = jnp.arange(occ_irreps.shape[0], dtype=jnp.int32)
    onehot = pair_list[:, :, None] == labels[None, None, :]
    picked = jnp.sum(jnp.where(onehot, occ_irreps[None, None, :], 0), axis=-1)
    return jnp.bitwise_xor(picked[:, 0], picked[:, 1])


def mask_amplitudes(amplitudes, win_irreps, symmetry):
    product = jnp.bitwise_xor(win_irreps[:, None], win_irreps[None, :])
    allowed = product[None, :, :] == symmetry[:, None, None]
    return jnp.where(allowed, amplitudes, jnp.zeros_like(amplitudes))


def gathered_body(factors, amplitudes, virt_irreps, win_irreps, occ_irreps, pair_list):
    per_device = factors.shape[1]
    n_rows = lax.axis_size("row")
    n_cols = lax.axis_size("col")
    block_a = per_device * n_cols
    slab = amplitudes.shape[0]
    symmetry = lookup_symmetry(occ_irreps, pair_list)
    own_symmetry = lax.dynamic_slice_in_dim(symmetry, lax.axis_index("pair") * slab, slab)
    every = lax.all_gather(amplitudes, "pair", axis=0, tiled=True)
    weights = mask_amplitudes(every, win_irreps, symmetry).astype(jnp.float32)
    n_fitting, _, width = factors.shape
    b_rows = lax.all_gather(factors, "row", axis=1, tiled=True)
    a_rows = lax.all_gather(factors, "col", axis=1, tiled=True)
    integral = lax.dot_general(
        a_rows.reshape(n_fitting, block_a * width),
        b_rows.reshape(n_fitting, n_rows * per_device * width),
        (((0,), (0,)), ((), ())),
        preferred_element_type=jnp.float32,
    )
    integral = integral.reshape(block_a, width, n_rows * per_device, width)
    part = jnp.einsum("acbd,pcd->pab", integral, weights, precision=lax.Precision.HIGHEST)
    full = lax.psum_scatter(part, "pair", scatter_dimension=0, tiled=True)
    full = full.reshape(slab, block_a, n_rows, per_device)
    a_labels = lax.dynamic_slice_in_dim(virt_irreps, lax.axis_index("row") * block_a, block_a)
    b_labels = lax.dynamic_slice_in_dim(
        virt_irreps.reshape(n_rows, -1), lax.axis_index("col") * per_device, per_device, 1
    )
    pair_sym = jnp.bitwise_xor(a_labels[:, None, None], b_labels[None, :, :])
    allowed = pair_sym[None, :, :, :] == own_symmetry[:, None, None, None]
    return jnp.where(allowed, full, 0.0)


def is_middle():
    col = lax.axis_index("col")
    return jnp.logical_or(col == 1, col == 2)


def one_hot(shape, wanted):
    first = lax.broadcasted_iota(jnp.int32, shape, 0)
    second = lax.broadcasted_iota(jnp.int32, shape, 1)
    return wanted(first, second).astype(jnp.bfloat16)


def multiply(left, right, dims):
    return lax.dot_general(left, right, dims, preferred_element_type=jnp.float32)


def pack_kernel(rest, own, out):
    n, n_fit = own.shape
    whole = n_fit - rest
    above = out.shape[0] - n
    turned = jnp.zeros((above, LANES), jnp.float32)
    for j in range(n // LANES):
        pick = one_hot((above, rest), lambda r, q: r == j * rest + q)
        turned = turned + multiply(pick, own[j * LANES : (j + 1) * LANES, whole:], NT)
    out[:above, :] = jnp.zeros((above, whole), jnp.bfloat16)
    out[:above, :LANES] = turned.astype(jnp.bfloat16)
    out[above:, :] = own[:, :whole]


def unpack(pieces, packed, rows, rest, segment=0):
    n, depth = rows.shape
    whole = depth - LANES
    to = 0
    for piece, start, count in pieces:
        rows[to : to + count, :whole] = piece[start : start + count, :]
        to += count
    tail = packed[: packed.shape[0] % LANES, :LANES]
    for j in range(n // LANES):
        base = (segment + j) * rest
        pick = one_hot(tail.shape, lambda r, q: jnp.logical_and(r == base + q, q < rest))
        rows[j * LANES : (j + 1) * LANES, whole:] = multiply(tail, pick, TN).astype(jnp.bfloat16)


def unpack_all(packed, rows, rest):
    unpack([(packed, packed.shape[0] % LANES, rows.shape[0])], packed, rows, rest)


def unpack_cut(first, second, rows, rest):
    above = first.shape[0] % LANES
    unpack([(first, above, first.shape[0] - above), (second, 0, second.shape[0])], first, rows, rest)


def window_major(width, per_device):
    n = width * per_device
    into = lax.broadcasted_iota(jnp.int32, (n, 1), 0)
    wanted = lax.rem(into, per_device) * width + lax.div(into, per_device)
    return (lax.broadcasted_iota(jnp.int32, (n, n), 1) == wanted).astype(jnp.bfloat16)


def place_rows(part, order, rows, k):
    width, _, per_device, depth = part.shape
    half = per_device // 2
    for h in range(2):
        moved = multiply(order, rows[h * half * width : (h + 1) * half * width, :], NN).astype(part.dtype)
        part[:, k : k + 1, h * half : (h + 1) * half] = moved.reshape(width, 1, half, depth)


def contract_block(rows, parts, weights, split, sums, keep, send, to=0):
    width, _, per_device, depth = parts[0].shape
    n_b = sum(part.shape[1] for part in parts) * per_device
    n_a = rows.shape[0] // width
    slab = keep.shape[0]
    n_p = weights.shape[0]

    def integrals(step, carry):
        pieces = [part[2 * step + j].reshape(-1, depth) for j in range(2) for part in parts]
        acc = multiply(rows[...], jnp.concatenate(pieces, axis=0), NT)
        high = acc.astype(jnp.bfloat16)
        low = (acc - high.astype(jnp.float32)).astype(jnp.bfloat16)
        for j in range(2):
            lanes = slice(j * n_b, (j + 1) * n_b)
            split[:n_a, 0, pl.ds(2 * step + j, 1)] = high[:, lanes].reshape(n_a, 1, width, n_b)
            split[:n_a, 1, pl.ds(2 * step + j, 1)] = low[:, lanes].reshape(n_a, 1, width, n_b)
        return carry

    lax.fori_loop(0, width // 2, integrals, 0, unroll=True)

    def ladder(step, carry):
        two = [split[2 * step + j].reshape(2 * width * width, n_b) for j in range(2)]
        res = multiply(weights[...], jnp.concatenate(two, axis=1), NN)
        for j in range(2):
            sums[pl.ds((2 * step + j) * n_p, n_p), :] = res[:, j * n_b : (j + 1) * n_b]
        return carry

    lax.fori_loop(0, n_a // 2, ladder, 0, unroll=True)
    for p in range(slab):
        keep[p, to : to + n_a] = sums[pl.ds(p, n_a, stride=n_p), :]
        send[p, to : to + n_a] = sums[pl.ds(n_p // 2 + p, n_a, stride=n_p), :]


def pair_symmetry(occ, pairs, p):
    return jnp.bitwise_xor(occ[pairs[0, p]], occ[pairs[1, p]])


def weight_rows(amplitudes, win, occ, pairs, place, n_p):
    width = amplitudes.shape[1]
    n = amplitudes.shape[0]
    slab = n // width
    first = place * slab
    lanes = width * width
    spread = multiply(amplitudes[...], one_hot((width, lanes), lambda d, l: d == lax.div(l, width)), NN)
    c_of_row = lax.rem(lax.broadcasted_iota(jnp.int32, (n, lanes), 0), width)
    c_of_lane = lax.rem(lax.broadcasted_iota(jnp.int32, (n, lanes), 1), width)
    spread = jnp.where(c_of_row == c_of_lane, spread, 0.0).astype(jnp.bfloat16)
    gathered = multiply(one_hot((n_p, n), lambda p, r: p == lax.div(r, width)), spread, NN)
    lane = lax.broadcasted_iota(jnp.int32, (n_p, lanes), 1)
    row = lax.broadcasted_iota(jnp.int32, (n_p, lanes), 0)
    product = jnp.zeros((n_p, lanes), jnp.int32)
    for w in range(width):
        label = win[w]
        product = jnp.bitwise_xor(product, jnp.where(lax.div(lane, width) == w, label, 0))
        product = jnp.bitwise_xor(product, jnp.where(lax.rem(lane, width) == w, label, 0))
    wanted = jnp.full((n_p, lanes), -1, jnp.int32)
    for p in range(slab):
        wanted = jnp.where(row == p, pair_symmetry(occ, pairs, first + p), wanted)
    masked = jnp.where(product == wanted, gathered, 0.0).astype(jnp.bfloat16)
    return jnp.concatenate([masked, masked], axis=1)


def prep_kernel(rest, own, by_core, mine, others, win, occ, pairs, part, own_rows, weights, held):
    width, _, per_device, _ = part.shape
    n_p = weights.shape[0] // 2
    pair = lax.axis_index("pair")
    weights[:n_p] = weight_rows(mine, win, occ, pairs, pair, n_p)
    weights[n_p:] = weight_rows(others, win, occ, pairs, 1 - pair, n_p)
    order = window_major(width, per_device // 2)
    for i, (packed, rows) in enumerate(((own, own_rows), (by_core, held))):
        unpack_all(packed, rows, rest)
        place_rows(part, order, rows, i)


def early_kernel(
    rest, own_rows, own_part, by_x, by_both, facing, weights, keep, send, x_part, held, split, sums
):
    width, _, per_device, _ = x_part.shape
    order = window_major(width, per_device // 2)
    for i, packed in enumerate((by_x, by_both)):
        unpack_all(packed, held, rest)
        place_rows(x_part, order, held, i)
    parts = (own_part, x_part)
    contract_block(own_rows, parts, weights, split, sums, keep.at[0], send.at[0])
    unpack_all(facing, held, rest)
    contract_block(held, parts, weights, split, sums, keep.at[1], send.at[1])


def outer_x_kernel(rest, passed_first, x_second, part, held):
    @pl.when(is_middle())
    def _():
        width, _, per_device, _ = part.shape
        unpack_cut(passed_first, x_second, held, rest)
        place_rows(part, window_major(width, per_device // 2), held, 0)


def outer_own_kernel(rest, facing, by_core, part, held):
    @pl.when(is_middle())
    def _():
        width, _, per_device, _ = part.shape
        order = window_major(width, per_device // 2)
        for i, packed in enumerate((facing, by_core)):
            unpack_all(packed, held, rest)
            place_rows(part, order, held, i)


def middle_kernel(rest, turned, own_part, x_part, weights, keep, send, held, split, sums):
    @pl.when(is_middle())
    def _():
        unpack_all(turned, held, rest)
        contract_block(held, (own_part, x_part), weights, split, sums, keep, send)


def late_kernel(
    rest, far_first, far_second, passed_first, passed_second, own_part, x_part, weights,
    keep, send, held, split, sums,
):
    middle = is_middle()

    @pl.when(middle)
    def _():
        unpack_cut(far_first, far_second, held, rest)

    @pl.when(jnp.logical_not(middle))
    def _():
        unpack_cut(passed_first, passed_second, held, rest)

    contract_block(held, (own_part, x_part), weights, split, sums, keep, send)


def across_kernel(rest, part, far_first, far_second, own, x, both, weights, keep, send, held, split, sums):
    @pl.when(is_middle())
    def _():
        above = far_first.shape[0] % LANES
        n = far_first.shape[0] - above
        if part:
            unpack([(far_second, 0, far_second.shape[0])], far_first, held, rest, n // LANES)
        else:
            unpack([(far_first, above, n)], far_first, held, rest)
        contract_block(held, (own, x, both), weights, split, sums, keep, send)


def add_kernel(keep_first, got_first, keep_second, got_second, out):
    n = keep_first.shape[1]
    out[:, :n] = keep_first[...] + got_first[...]
    out[:, n:] = keep_second[...] + got_second[...]


def finish_kernel(
    virt, occ, pairs, keep_early, got_early, keep_middle, got_middle, keep_late, got_late, across, out, whole
):
    row = lax.axis_index("row")
    col = lax.axis_index("col")
    middle = is_middle()
    lower = col < 2
    n_p, n_a, n_b = across.shape
    planes = (col, jnp.bitwise_xor(col, 1), jnp.where(lower, 2, 1), jnp.where(lower, 3, 0))

    def place(s):
        return pl.ds(pl.multiple_of(planes[s] * n_a, n_a), n_a)

    for s in range(2):
        whole[:, place(s), :] = keep_early[s] + got_early[s]

    @pl.when(middle)
    def _():
        whole[:, place(2), :] = keep_middle[...] + got_middle[...]
        whole[:, place(3), :] = keep_late[...] + got_late[...]

    @pl.when(jnp.logical_not(middle))
    def _():
        whole[:, place(2), :] = keep_late[...] + got_late[...]
        whole[:, place(3), :] = across[...]

    n_rows, block_a = virt.shape
    rows = [jnp.bitwise_xor(row, i) for i in range(n_rows)]
    spread = [jnp.broadcast_to(virt[pl.ds(k, 1), :], (n_a, block_a)) for k in rows]
    lane = lax.broadcasted_iota(jnp.int32, (n_b, block_a), 1)
    place_b = lax.rem(lax.broadcasted_iota(jnp.int32, (n_b, 1), 0), n_a) + col * n_a
    b_labels = jnp.sum(jnp.where(lane == place_b, jnp.concatenate(spread, axis=0), 0), axis=1, keepdims=True)
    pair_sym = jnp.bitwise_xor(b_labels, virt[pl.ds(row, 1), :])
    first = lax.axis_index("pair") * n_p
    for p in range(n_p):
        masked = jnp.where(pair_sym == pair_symmetry(occ, pairs, first + p), whole[p].T, 0.0)
        for i, k in enumerate(rows):
            out[p, pl.ds(pl.multiple_of(k * n_a, n_a), n_a), :] = masked[i * n_a : (i + 1) * n_a]


def swap(array, axis, mask):
    size = lax.axis_size(axis)
    return lax.ppermute(array, axis, [(i, i ^ mask) for i in range(size)])


def staged_body(factors, amplitudes, virt_irreps, win_irreps, occ_irreps, pair_list):
    n_fit, per_device, width = factors.shape
    n_rows = lax.axis_size("row")
    n_cols = lax.axis_size("col")
    n_pair = lax.axis_size("pair")
    n_b = n_rows * per_device
    block_a = per_device * n_cols
    slab = amplitudes.shape[0]
    n = per_device * width
    rest = n_fit % LANES
    below = 16 * pl.cdiv(rest * (n // LANES), 16)
    depth = n_fit - rest + LANES
    n_p = 16 * pl.cdiv(slab, 16)

    vmem = pl.BlockSpec(memory_space=pltpu.VMEM)
    smem = pl.BlockSpec(memory_space=pltpu.SMEM)

    def array(*shape, dtype=jnp.bfloat16):
        return jax.ShapeDtypeStruct(shape, dtype)

    def sums_of(*shape):
        return array(*shape, n_b, dtype=jnp.float32)

    def panel(count):
        return array(width, count, per_device, depth)

    held = pltpu.VMEM((n, depth), jnp.bfloat16)
    work = [
        pltpu.VMEM((per_device, 2, width, width, n_b), jnp.bfloat16),
        pltpu.VMEM((per_device * 2 * n_p, n_b), jnp.float32),
    ]

    def call(kernel, name, out_shape, in_specs, out_specs, scratch, n_blocks=None):
        estimate = None
        if n_blocks is not None:
            flops = int(20 * n_blocks * n * n_b * width * depth)
            estimate = pl.CostEstimate(flops=flops, bytes_accessed=8 * n * depth, transcendentals=0)
        return pl.pallas_call(
            kernel,
            out_shape=out_shape,
            in_specs=in_specs,
            out_specs=out_specs,
            scratch_shapes=scratch,
            compiler_params=pltpu.CompilerParams(vmem_limit_bytes=VMEM_LIMIT),
            cost_estimate=estimate,
            name=name,
        )

    def permute(x, to):
        pairs = [
            (r * n_cols + c, to_r * n_cols + to_c)
            for r in range(n_rows)
            for c in range(n_cols)
            for to_r, to_c in [to(r, c, c in (1, 2))]
        ]
        return lax.ppermute(x, ("row", "col"), pairs)

    def face(x):
        return permute(x, lambda r, c, middle: (r, c ^ 1))

    def turn(x):
        return permute(x, lambda r, c, middle: (r, 3 - c) if middle else (r ^ 2, c))

    def cross(x):
        return permute(x, lambda r, c, middle: (r, 3 - c) if middle else (r ^ 1, c))

    def along_x(x):
        return permute(x, lambda r, c, middle: (r ^ 2, c) if middle else (r ^ 1, c))

    def core(x):
        return permute(x, lambda r, c, middle: (r ^ 1, c))

    def after(x, *others):
        return lax.optimization_barrier((x, *others))[0]

    own = call(
        lambda *refs: pack_kernel(rest, *refs), "pack", array(n + below, n_fit - rest), [vmem], vmem, []
    )(jnp.transpose(factors, (1, 2, 0)).reshape(n, n_fit))

    turned = turn(own)
    facing = face(own)
    by_x = along_x(own)
    by_core = core(own)
    others = swap(amplitudes, "pair", 1)

    pairs = jnp.transpose(pair_list)
    own_part, own_rows, weights = call(
        lambda *refs: prep_kernel(rest, *refs),
        "prep",
        (panel(2), array(n, depth), array(2 * n_p, 2 * width * width)),
        [vmem] * 4 + [smem] * 3,
        (vmem,) * 3,
        [held],
        1,
    )(
        own, by_core,
        amplitudes.reshape(slab * width, width), others.reshape(slab * width, width),
        win_irreps, occ_irreps, pairs,
    )

    def cut(x, where):
        return x[: below + where], x[below + where :]

    facing_first, facing_second = cut(facing, 3 * n // 4)
    turned_first, turned_second = cut(turned, n // 2)
    passed_first = face(turned_first)
    far_first = cross(facing_first)
    x_second = along_x(cut(facing, n // 2)[1])
    x_rows = jnp.where(is_middle(), by_x, turned)
    by_both = core(x_rows)
    facing_core = core(facing)

    own_panel = call(
        lambda *refs: outer_own_kernel(rest, *refs), "outer_own", panel(2), [vmem] * 2, vmem, [held], 0.2
    )(facing, facing_core)
    far_second = cross(after(facing_second, own_panel))
    passed_second = face(after(turned_second, own_panel))
    early = sums_of(2, slab, per_device)
    keep_early, send_early, x_part = call(
        lambda *refs: early_kernel(rest, *refs),
        "early",
        (early, early, panel(2)),
        [vmem] * 6,
        (vmem,) * 3,
        [held, *work],
        2,
    )(after(own_rows, own_panel), own_part, x_rows, by_both, facing, weights)
    got_early = swap(send_early, "pair", 1)

    x_panel = call(
        lambda *refs: outer_x_kernel(rest, *refs), "outer_x", panel(1), [vmem] * 2, vmem, [held], 0.0
    )(after(passed_first, keep_early), x_second)
    both_panel = core(x_panel)

    block = sums_of(slab, per_device)
    keep_middle, send_middle = call(
        lambda *refs: middle_kernel(rest, *refs), "middle", (block, block), [vmem] * 4, (vmem, vmem), [held, *work], 0.65
    )(turned, own_part, after(x_part, x_panel), weights)
    got_middle = swap(send_middle, "pair", 1)

    def across(part, both):
        count = (far_second if part else far_first).shape[0] // LANES * LANES
        sums = sums_of(slab, count // width)
        keep, send = call(
            lambda *refs: across_kernel(rest, part, *refs),
            "across",
            (sums, sums),
            [vmem] * 6,
            (vmem, vmem),
            [pltpu.VMEM((count, depth), jnp.bfloat16), *work],
            0.0,
        )(far_first, far_second if part else far_first, own_panel, x_panel, both, weights)
        return keep, send, swap(send, "pair", 1)

    keep_across, send_across, got_across = across(0, after(both_panel, keep_middle))
    keep_again, send_again, got_again = across(1, after(both_panel, keep_across, got_early))

    keep_late, send_late = call(
        lambda *refs: late_kernel(rest, *refs),
        "late",
        (block, block),
        [vmem] * 7,
        (vmem, vmem),
        [held, *work],
        0.1,
    )(far_first, far_second, passed_first, passed_second, own_part, after(x_part, keep_again, got_middle), weights)
    got_late = swap(send_late, "pair", 1)
    summed = call(add_kernel, "add", sums_of(slab, per_device), [vmem] * 4, vmem, [])(
        keep_across, got_across, keep_again, got_again
    )
    outwards = face(summed)

    out = call(
        finish_kernel,
        "finish",
        sums_of(slab, block_a),
        [vmem] + [smem] * 2 + [vmem] * 7,
        vmem,
        [pltpu.VMEM((slab, block_a, n_b), jnp.float32)],
    )(
        virt_irreps.reshape(n_rows, block_a), occ_irreps, pairs,
        keep_early, got_early, keep_middle, got_middle, keep_late, got_late, outwards,
    )
    return jnp.transpose(out.reshape(slab, n_rows, per_device, block_a), (0, 3, 1, 2))


def solution(mesh):
    staged = (mesh.shape["row"], mesh.shape["col"], mesh.shape["pair"]) == (4, 4, 2)
    body = staged_body if staged else gathered_body
    in_specs = (P("pair", ("row", "col"), None), P("pair", None, None), P(), P(), P(), P())
    out_specs = P("pair", "row", None, "col")
    return jax.shard_map(body, mesh=mesh, in_specs=in_specs, out_specs=out_specs, check_vma=False)
```

```python
import jax
import jax.numpy as jnp
from jax import lax
from jax.experimental import pallas as pl
from jax.experimental.pallas import tpu as pltpu
from jax.sharding import PartitionSpec as P

VMEM_LIMIT = 16 * 1024 * 1024
LANES = 128
NT = (((1,), (1,)), ((), ()))
NN = (((1,), (0,)), ((), ()))
TN = (((0,), (0,)), ((), ()))


def lookup_symmetry(occ_irreps, pair_list):
    labels = jnp.arange(occ_irreps.shape[0], dtype=jnp.int32)
    onehot = pair_list[:, :, None] == labels[None, None, :]
    picked = jnp.sum(jnp.where(onehot, occ_irreps[None, None, :], 0), axis=-1)
    return jnp.bitwise_xor(picked[:, 0], picked[:, 1])


def mask_amplitudes(amplitudes, win_irreps, symmetry):
    product = jnp.bitwise_xor(win_irreps[:, None], win_irreps[None, :])
    allowed = product[None, :, :] == symmetry[:, None, None]
    return jnp.where(allowed, amplitudes, jnp.zeros_like(amplitudes))


def gathered_body(factors, amplitudes, virt_irreps, win_irreps, occ_irreps, pair_list):
    per_device = factors.shape[1]
    n_rows = lax.axis_size("row")
    n_cols = lax.axis_size("col")
    block_a = per_device * n_cols
    slab = amplitudes.shape[0]
    symmetry = lookup_symmetry(occ_irreps, pair_list)
    own_symmetry = lax.dynamic_slice_in_dim(symmetry, lax.axis_index("pair") * slab, slab)
    every = lax.all_gather(amplitudes, "pair", axis=0, tiled=True)
    weights = mask_amplitudes(every, win_irreps, symmetry).astype(jnp.float32)
    n_fitting, _, width = factors.shape
    b_rows = lax.all_gather(factors, "row", axis=1, tiled=True)
    a_rows = lax.all_gather(factors, "col", axis=1, tiled=True)
    integral = lax.dot_general(
        a_rows.reshape(n_fitting, block_a * width),
        b_rows.reshape(n_fitting, n_rows * per_device * width),
        (((0,), (0,)), ((), ())),
        preferred_element_type=jnp.float32,
    )
    integral = integral.reshape(block_a, width, n_rows * per_device, width)
    part = jnp.einsum("acbd,pcd->pab", integral, weights, precision=lax.Precision.HIGHEST)
    full = lax.psum_scatter(part, "pair", scatter_dimension=0, tiled=True)
    full = full.reshape(slab, block_a, n_rows, per_device)
    a_labels = lax.dynamic_slice_in_dim(virt_irreps, lax.axis_index("row") * block_a, block_a)
    b_labels = lax.dynamic_slice_in_dim(
        virt_irreps.reshape(n_rows, -1), lax.axis_index("col") * per_device, per_device, 1
    )
    pair_sym = jnp.bitwise_xor(a_labels[:, None, None], b_labels[None, :, :])
    allowed = pair_sym[None, :, :, :] == own_symmetry[:, None, None, None]
    return jnp.where(allowed, full, 0.0)


def is_middle():
    col = lax.axis_index("col")
    return jnp.logical_or(col == 1, col == 2)


def one_hot(shape, wanted):
    first = lax.broadcasted_iota(jnp.int32, shape, 0)
    second = lax.broadcasted_iota(jnp.int32, shape, 1)
    return wanted(first, second).astype(jnp.bfloat16)


def multiply(left, right, dims):
    return lax.dot_general(left, right, dims, preferred_element_type=jnp.float32)


def pack_kernel(rest, own, out):
    n, n_fit = own.shape
    whole = n_fit - rest
    above = out.shape[0] - n
    turned = jnp.zeros((above, LANES), jnp.float32)
    for j in range(n // LANES):
        pick = one_hot((above, rest), lambda r, q: r == j * rest + q)
        turned = turned + multiply(pick, own[j * LANES : (j + 1) * LANES, whole:], NT)
    out[:above, :] = jnp.zeros((above, whole), jnp.bfloat16)
    out[:above, :LANES] = turned.astype(jnp.bfloat16)
    out[above:, :] = own[:, :whole]


def unpack(pieces, packed, rows, rest, segment=0):
    n, depth = rows.shape
    whole = depth - LANES
    to = 0
    for piece, start, count in pieces:
        rows[to : to + count, :whole] = piece[start : start + count, :]
        to += count
    tail = packed[: packed.shape[0] % LANES, :LANES]
    for j in range(n // LANES):
        base = (segment + j) * rest
        pick = one_hot(tail.shape, lambda r, q: jnp.logical_and(r == base + q, q < rest))
        rows[j * LANES : (j + 1) * LANES, whole:] = multiply(tail, pick, TN).astype(jnp.bfloat16)


def unpack_all(packed, rows, rest):
    unpack([(packed, packed.shape[0] % LANES, rows.shape[0])], packed, rows, rest)


def unpack_cut(first, second, rows, rest):
    above = first.shape[0] % LANES
    unpack([(first, above, first.shape[0] - above), (second, 0, second.shape[0])], first, rows, rest)


def window_major(width, per_device):
    n = width * per_device
    into = lax.broadcasted_iota(jnp.int32, (n, 1), 0)
    wanted = lax.rem(into, per_device) * width + lax.div(into, per_device)
    return (lax.broadcasted_iota(jnp.int32, (n, n), 1) == wanted).astype(jnp.bfloat16)


def place_rows(part, order, rows, k):
    width, _, per_device, depth = part.shape
    half = per_device // 2
    for h in range(2):
        moved = multiply(order, rows[h * half * width : (h + 1) * half * width, :], NN).astype(part.dtype)
        part[:, k : k + 1, h * half : (h + 1) * half] = moved.reshape(width, 1, half, depth)


def contract_block(rows, parts, weights, split, sums, keep, send, to=0):
    width, _, per_device, depth = parts[0].shape
    n_b = sum(part.shape[1] for part in parts) * per_device
    n_a = rows.shape[0] // width
    slab = keep.shape[0]
    n_p = weights.shape[0]

    def integrals(step, carry):
        pieces = [part[2 * step + j].reshape(-1, depth) for j in range(2) for part in parts]
        acc = multiply(rows[...], jnp.concatenate(pieces, axis=0), NT)
        high = acc.astype(jnp.bfloat16)
        low = (acc - high.astype(jnp.float32)).astype(jnp.bfloat16)
        for j in range(2):
            lanes = slice(j * n_b, (j + 1) * n_b)
            split[:n_a, 0, pl.ds(2 * step + j, 1)] = high[:, lanes].reshape(n_a, 1, width, n_b)
            split[:n_a, 1, pl.ds(2 * step + j, 1)] = low[:, lanes].reshape(n_a, 1, width, n_b)
        return carry

    lax.fori_loop(0, width // 2, integrals, 0, unroll=True)

    def ladder(step, carry):
        two = [split[2 * step + j].reshape(2 * width * width, n_b) for j in range(2)]
        res = multiply(weights[...], jnp.concatenate(two, axis=1), NN)
        for j in range(2):
            sums[pl.ds((2 * step + j) * n_p, n_p), :] = res[:, j * n_b : (j + 1) * n_b]
        return carry

    lax.fori_loop(0, n_a // 2, ladder, 0, unroll=True)
    for p in range(slab):
        keep[p, to : to + n_a] = sums[pl.ds(p, n_a, stride=n_p), :]
        send[p, to : to + n_a] = sums[pl.ds(n_p // 2 + p, n_a, stride=n_p), :]


def pair_symmetry(occ, pairs, p):
    return jnp.bitwise_xor(occ[pairs[0, p]], occ[pairs[1, p]])


def weight_rows(amplitudes, win, occ, pairs, place, n_p):
    width = amplitudes.shape[1]
    n = amplitudes.shape[0]
    slab = n // width
    first = place * slab
    lanes = width * width
    spread = multiply(amplitudes[...], one_hot((width, lanes), lambda d, l: d == lax.div(l, width)), NN)
    c_of_row = lax.rem(lax.broadcasted_iota(jnp.int32, (n, lanes), 0), width)
    c_of_lane = lax.rem(lax.broadcasted_iota(jnp.int32, (n, lanes), 1), width)
    spread = jnp.where(c_of_row == c_of_lane, spread, 0.0).astype(jnp.bfloat16)
    gathered = multiply(one_hot((n_p, n), lambda p, r: p == lax.div(r, width)), spread, NN)
    lane = lax.broadcasted_iota(jnp.int32, (n_p, lanes), 1)
    row = lax.broadcasted_iota(jnp.int32, (n_p, lanes), 0)
    product = jnp.zeros((n_p, lanes), jnp.int32)
    for w in range(width):
        label = win[w]
        product = jnp.bitwise_xor(product, jnp.where(lax.div(lane, width) == w, label, 0))
        product = jnp.bitwise_xor(product, jnp.where(lax.rem(lane, width) == w, label, 0))
    wanted = jnp.full((n_p, lanes), -1, jnp.int32)
    for p in range(slab):
        wanted = jnp.where(row == p, pair_symmetry(occ, pairs, first + p), wanted)
    masked = jnp.where(product == wanted, gathered, 0.0).astype(jnp.bfloat16)
    return jnp.concatenate([masked, masked], axis=1)


def prep_kernel(rest, own, by_core, mine, others, win, occ, pairs, part, own_rows, weights, held):
    width, _, per_device, _ = part.shape
    n_p = weights.shape[0] // 2
    pair = lax.axis_index("pair")
    weights[:n_p] = weight_rows(mine, win, occ, pairs, pair, n_p)
    weights[n_p:] = weight_rows(others, win, occ, pairs, 1 - pair, n_p)
    order = window_major(width, per_device // 2)
    for i, (packed, rows) in enumerate(((own, own_rows), (by_core, held))):
        unpack_all(packed, rows, rest)
        place_rows(part, order, rows, i)


def early_kernel(
    rest, own_rows, own_part, by_x, by_both, facing, weights, keep, send, x_part, held, split, sums
):
    width, _, per_device, _ = x_part.shape
    order = window_major(width, per_device // 2)
    for i, packed in enumerate((by_x, by_both)):
        unpack_all(packed, held, rest)
        place_rows(x_part, order, held, i)
    parts = (own_part, x_part)
    contract_block(own_rows, parts, weights, split, sums, keep.at[0], send.at[0])
    unpack_all(facing, held, rest)
    contract_block(held, parts, weights, split, sums, keep.at[1], send.at[1])


def pick_kernel(by_x, turned, out):
    middle = is_middle()

    @pl.when(middle)
    def _():
        out[...] = by_x[...]

    @pl.when(jnp.logical_not(middle))
    def _():
        out[...] = turned[...]


def outer_x_kernel(rest, passed_first, x_second, part, held):
    @pl.when(is_middle())
    def _():
        width, _, per_device, _ = part.shape
        unpack_cut(passed_first, x_second, held, rest)
        place_rows(part, window_major(width, per_device // 2), held, 0)


def outer_own_kernel(rest, facing, by_core, part, held):
    @pl.when(is_middle())
    def _():
        width, _, per_device, _ = part.shape
        order = window_major(width, per_device // 2)
        for i, packed in enumerate((facing, by_core)):
            unpack_all(packed, held, rest)
            place_rows(part, order, held, i)


def middle_kernel(rest, turned, own_part, x_part, weights, keep, send, held, split, sums):
    @pl.when(is_middle())
    def _():
        unpack_all(turned, held, rest)
        contract_block(held, (own_part, x_part), weights, split, sums, keep, send)


def late_near_kernel(
    rest, far_first, far_second, passed_first, own_part, x_part, weights, keep, send, held, split, sums
):
    middle = is_middle()
    parts = (own_part, x_part)

    @pl.when(middle)
    def _():
        unpack_cut(far_first, far_second, held, rest)
        contract_block(held, parts, weights, split, sums, keep, send)

    @pl.when(jnp.logical_not(middle))
    def _():
        above = passed_first.shape[0] % LANES
        n = passed_first.shape[0] - above
        rows = held.at[pl.ds(0, n)]
        unpack([(passed_first, above, n)], passed_first, rows, rest)
        contract_block(rows, parts, weights, split, sums, keep, send)


def late_last_kernel(
    rest, passed_first, passed_second, keep_near, send_near, own_part, x_part, weights, keep, send, held, split, sums
):
    keep[...] = keep_near[...]
    send[...] = send_near[...]

    @pl.when(jnp.logical_not(is_middle()))
    def _():
        n = passed_second.shape[0]
        segment = (passed_first.shape[0] - passed_first.shape[0] % LANES) // LANES
        rows = held.at[pl.ds(0, n)]
        unpack([(passed_second, 0, n)], passed_first, rows, rest, segment)
        to = keep.shape[1] - n // own_part.shape[0]
        contract_block(rows, (own_part, x_part), weights, split, sums, keep, send, to)


def across_first_kernel(rest, far_first, own, x, both, weights, keep, send, held, split, sums):
    @pl.when(is_middle())
    def _():
        unpack_all(far_first, held, rest)
        contract_block(held, (own, x, both), weights, split, sums, keep, send)


def across_second_kernel(
    rest, far_first, far_second, own, x, both, weights, keep_first, send_first, keep, send, held, split, sums
):
    @pl.when(is_middle())
    def _():
        n_a = keep_first.shape[1]
        keep[:, :n_a] = keep_first[...]
        send[:, :n_a] = send_first[...]
        above = far_first.shape[0] % LANES
        segment = (far_first.shape[0] - above) // LANES
        unpack([(far_second, 0, far_second.shape[0])], far_first, held, rest, segment)
        contract_block(held, (own, x, both), weights, split, sums, keep, send, n_a)


def add_kernel(keep, got, out):
    out[...] = keep[...] + got[...]


def finish_kernel(
    virt, occ, pairs, keep_early, got_early, keep_middle, got_middle, keep_late, got_late, across, out, whole
):
    row = lax.axis_index("row")
    col = lax.axis_index("col")
    middle = is_middle()
    lower = col < 2
    n_p, n_a, n_b = across.shape
    planes = (col, jnp.bitwise_xor(col, 1), jnp.where(lower, 2, 1), jnp.where(lower, 3, 0))

    def place(s):
        return pl.ds(pl.multiple_of(planes[s] * n_a, n_a), n_a)

    for s in range(2):
        whole[:, place(s), :] = keep_early[s] + got_early[s]

    @pl.when(middle)
    def _():
        whole[:, place(2), :] = keep_middle[...] + got_middle[...]
        whole[:, place(3), :] = keep_late[...] + got_late[...]

    @pl.when(jnp.logical_not(middle))
    def _():
        whole[:, place(2), :] = keep_late[...] + got_late[...]
        whole[:, place(3), :] = across[...]

    n_rows, block_a = virt.shape
    rows = [jnp.bitwise_xor(row, i) for i in range(n_rows)]
    spread = [jnp.broadcast_to(virt[pl.ds(k, 1), :], (n_a, block_a)) for k in rows]
    lane = lax.broadcasted_iota(jnp.int32, (n_b, block_a), 1)
    place_b = lax.rem(lax.broadcasted_iota(jnp.int32, (n_b, 1), 0), n_a) + col * n_a
    b_labels = jnp.sum(jnp.where(lane == place_b, jnp.concatenate(spread, axis=0), 0), axis=1, keepdims=True)
    pair_sym = jnp.bitwise_xor(b_labels, virt[pl.ds(row, 1), :])
    first = lax.axis_index("pair") * n_p
    for p in range(n_p):
        masked = jnp.where(pair_sym == pair_symmetry(occ, pairs, first + p), whole[p].T, 0.0)
        for i, k in enumerate(rows):
            out[p, pl.ds(pl.multiple_of(k * n_a, n_a), n_a), :] = masked[i * n_a : (i + 1) * n_a]


def swap(array, axis, mask):
    size = lax.axis_size(axis)
    return lax.ppermute(array, axis, [(i, i ^ mask) for i in range(size)])


def staged_body(factors, amplitudes, virt_irreps, win_irreps, occ_irreps, pair_list):
    n_fit, per_device, width = factors.shape
    n_rows = lax.axis_size("row")
    n_cols = lax.axis_size("col")
    n_pair = lax.axis_size("pair")
    n_b = n_rows * per_device
    block_a = per_device * n_cols
    slab = amplitudes.shape[0]
    n = per_device * width
    rest = n_fit % LANES
    below = 16 * pl.cdiv(rest * (n // LANES), 16)
    depth = n_fit - rest + LANES
    n_p = 16 * pl.cdiv(slab, 16)

    vmem = pl.BlockSpec(memory_space=pltpu.VMEM)
    smem = pl.BlockSpec(memory_space=pltpu.SMEM)

    def array(*shape, dtype=jnp.bfloat16):
        return jax.ShapeDtypeStruct(shape, dtype)

    def sums_of(*shape):
        return array(*shape, n_b, dtype=jnp.float32)

    def panel(count):
        return array(width, count, per_device, depth)

    held = pltpu.VMEM((n, depth), jnp.bfloat16)
    work = [
        pltpu.VMEM((per_device, 2, width, width, n_b), jnp.bfloat16),
        pltpu.VMEM((per_device * 2 * n_p, n_b), jnp.float32),
    ]

    def call(kernel, name, out_shape, in_specs, out_specs, scratch, n_blocks=None):
        estimate = None
        if n_blocks is not None:
            flops = int(20 * n_blocks * n * n_b * width * depth)
            estimate = pl.CostEstimate(flops=flops, bytes_accessed=8 * n * depth, transcendentals=0)
        return pl.pallas_call(
            kernel,
            out_shape=out_shape,
            in_specs=in_specs,
            out_specs=out_specs,
            scratch_shapes=scratch,
            compiler_params=pltpu.CompilerParams(vmem_limit_bytes=VMEM_LIMIT),
            cost_estimate=estimate,
            name=name,
        )

    def permute(x, to):
        pairs = [
            (r * n_cols + c, to_r * n_cols + to_c)
            for r in range(n_rows)
            for c in range(n_cols)
            for to_r, to_c in [to(r, c, c in (1, 2))]
        ]
        return lax.ppermute(x, ("row", "col"), pairs)

    def face(x):
        return permute(x, lambda r, c, middle: (r, c ^ 1))

    def turn(x):
        return permute(x, lambda r, c, middle: (r, 3 - c) if middle else (r ^ 2, c))

    def cross(x):
        return permute(x, lambda r, c, middle: (r, 3 - c) if middle else (r ^ 1, c))

    def along_x(x):
        return permute(x, lambda r, c, middle: (r ^ 2, c) if middle else (r ^ 1, c))

    def core(x):
        return permute(x, lambda r, c, middle: (r ^ 1, c))

    def after(x, *others):
        return lax.optimization_barrier((x, *others))[0]

    own = call(
        lambda *refs: pack_kernel(rest, *refs), "pack", array(n + below, n_fit - rest), [vmem], vmem, []
    )(jnp.transpose(factors, (1, 2, 0)).reshape(n, n_fit))

    turned = turn(own)
    facing = face(own)
    by_x = along_x(own)
    by_core = core(own)
    others = swap(amplitudes, "pair", 1)

    pairs = jnp.transpose(pair_list)
    own_part, own_rows, weights = call(
        lambda *refs: prep_kernel(rest, *refs),
        "prep",
        (panel(2), array(n, depth), array(2 * n_p, 2 * width * width)),
        [vmem] * 4 + [smem] * 3,
        (vmem,) * 3,
        [held],
        1,
    )(
        own, by_core,
        amplitudes.reshape(slab * width, width), others.reshape(slab * width, width),
        win_irreps, occ_irreps, pairs,
    )

    def cut(x, where):
        return x[: below + where], x[below + where :]

    facing_first, facing_second = cut(facing, 3 * n // 4)
    turned_first, turned_second = cut(turned, n // 2)
    passed_first = face(turned_first)
    far_first = cross(facing_first)
    x_second = along_x(cut(facing, n // 2)[1])
    x_rows = call(pick_kernel, "pick", array(n + below, n_fit - rest), [vmem] * 2, vmem, [])(by_x, turned)
    by_both = core(x_rows)
    facing_core = core(facing)

    own_panel = call(
        lambda *refs: outer_own_kernel(rest, *refs), "outer_own", panel(2), [vmem] * 2, vmem, [held], 0.0
    )(facing, facing_core)
    far_second = cross(after(facing_second, own_panel))
    passed_second = face(after(turned_second, own_panel))
    early = sums_of(2, slab, per_device)
    keep_early, send_early, x_part = call(
        lambda *refs: early_kernel(rest, *refs),
        "early",
        (early, early, panel(2)),
        [vmem] * 6,
        (vmem,) * 3,
        [held, *work],
        0.1,
    )(after(own_rows, own_panel), own_part, x_rows, by_both, facing, weights)
    got_early = swap(send_early, "pair", 1)

    x_panel = call(
        lambda *refs: outer_x_kernel(rest, *refs), "outer_x", panel(1), [vmem] * 2, vmem, [held], 0.0
    )(after(passed_first, keep_early), x_second)
    both_panel = core(x_panel)

    block = sums_of(slab, per_device)
    keep_middle, send_middle = call(
        lambda *refs: middle_kernel(rest, *refs), "middle", (block, block), [vmem] * 4, (vmem, vmem), [held, *work], 0.65
    )(turned, own_part, after(x_part, x_panel), weights)
    got_middle = swap(send_middle, "pair", 1)

    def rows(x):
        return x.shape[0] // LANES * LANES

    part = sums_of(slab, rows(far_first) // width)
    keep_first, send_first = call(
        lambda *refs: across_first_kernel(rest, *refs),
        "across_first",
        (part, part),
        [vmem] * 5,
        (vmem, vmem),
        [pltpu.VMEM((rows(far_first), depth), jnp.bfloat16), *work],
        0.0,
    )(far_first, own_panel, x_panel, after(both_panel, keep_middle), weights)
    keep_across, send_across = call(
        lambda *refs: across_second_kernel(rest, *refs),
        "across_second",
        (block, block),
        [vmem] * 8,
        (vmem, vmem),
        [pltpu.VMEM((rows(far_second), depth), jnp.bfloat16), *work],
        0.0,
    )(far_first, far_second, own_panel, x_panel, after(both_panel, keep_first, got_early), weights, keep_first, send_first)
    got_across = swap(send_across, "pair", 1)

    keep_near, send_near = call(
        lambda *refs: late_near_kernel(rest, *refs),
        "late_near",
        (block, block),
        [vmem] * 6,
        (vmem, vmem),
        [held, *work],
        0.1,
    )(far_first, far_second, passed_first, own_part, after(x_part, keep_across), weights)
    keep_late, send_late = call(
        lambda *refs: late_last_kernel(rest, *refs),
        "late_last",
        (block, block),
        [vmem] * 7,
        (vmem, vmem),
        [held, *work],
        0.1,
    )(passed_first, passed_second, keep_near, send_near, own_part, x_part, weights)
    got_late = swap(send_late, "pair", 1)
    summed = call(add_kernel, "add", block, [vmem] * 2, vmem, [])(keep_across, got_across)
    outwards = face(summed)

    out = call(
        finish_kernel,
        "finish",
        sums_of(slab, block_a),
        [vmem] + [smem] * 2 + [vmem] * 7,
        vmem,
        [pltpu.VMEM((slab, block_a, n_b), jnp.float32)],
    )(
        virt_irreps.reshape(n_rows, block_a), occ_irreps, pairs,
        keep_early, got_early, keep_middle, got_middle, keep_late, got_late, outwards,
    )
    return jnp.transpose(out.reshape(slab, n_rows, per_device, block_a), (0, 3, 1, 2))


def solution(mesh):
    staged = (mesh.shape["row"], mesh.shape["col"], mesh.shape["pair"]) == (4, 4, 2)
    body = staged_body if staged else gathered_body
    in_specs = (P("pair", ("row", "col"), None), P("pair", None, None), P(), P(), P(), P())
    out_specs = P("pair", "row", None, "col")
    return jax.shard_map(body, mesh=mesh, in_specs=in_specs, out_specs=out_specs, check_vma=False)
```
